128 devices in a mesh: seq: 16 (over x, y), head: 8 (over z, core).
Axes of the slice: x: 4, y: 4, z: 4, core: 2. Of those that a mesh axis runs over, the one named last changes fastest.
Arguments:
- attn_queries: float32 [4096, 4096], P('seq', 'head'), may hold values from -6 to 6
- attn_keys: float32 [4096, 4096], P('seq', 'head'), may hold values from -6 to 6
- attn_values: float32 [4096, 4096], P('seq', 'head'), may hold values from -6 to 6
- head_gain: float32 [128], replicated, may hold values from 0.25 to 1.75
- out_weight: bfloat16 [4096, 2048], P('head'), may hold values from -0.09375 to 0.09375
- residual_in: bfloat16 [4096, 2048], P(('seq', 'head')), may hold values from -6 to 6
- norm_gain: float32 [2048], replicated, may hold values from 0.25 to 1.75
- routed_experts: int32 [4096, 8], P(('seq', 'head')), may hold values from 0 to 127, all different within a row; in each aligned block of 32 rows (0 to 31, 32 to 63, ...) at most 5 rows name the same one
- gate_weights: float32 [4096, 8], P(('seq', 'head')), may hold values from 0.05 to 1
- expert_gate: bfloat16 [128, 2048, 768], P(('seq', 'head')), may hold values from -0.125 to 0.125
- expert_up: bfloat16 [128, 2048, 768], P(('seq', 'head')), may hold values from -0.125 to 0.125
- expert_down: bfloat16 [128, 768, 2048], P(('seq', 'head')), may hold values from -0.21875 to 0.21875
Outputs:
- attn_out: bfloat16 [4096, 2048], P(('seq', 'head'))
- moe_out: bfloat16 [4096, 2048], P(('seq', 'head'))
The draws below stay inside these ranges and needn't reach their ends.
Inputs may be any that keep to these rules, and one draw needn't show every extreme that they name: `routed_experts`: the 8 experts of a token differ. In each aligned block of 32 rows no expert is named by more than 5 rows, and in some block one expert is named by exactly 5 rows.
All inputs are finite; a program needn't handle non-finite values.
Results may differ from the reference program's by a relative error of at most 0.03.
Values may be sent and summed in bfloat16 or wider, within the bound.
No kernel may reach another device: no remote copies, remote signals or barrier semaphores. Data moves between devices by JAX's collectives and lax.ppermute only.
A program may use at most 64 MiB of HBM per device.

```python
import math
import jax
import jax.numpy as jnp
import numpy as np
from jax import lax

D = 2048
HEADS = 32
HD = 128
FF = 768
TOPK = 8
TOKENS = 4096
ROWS_DEV = 32
EXPERTS = 128
CAP = 5


def block_levels(own_key, extent, shards, least, high):
    gain, own = 1.0, jax.random.fold_in(own_key, 6)
    for position, parts in shards:
        heights = jnp.exp(jax.random.uniform(jax.random.fold_in(own, position), (parts,), jnp.float32, least / len(shards), high / len(shards)))
        gain = gain * jnp.repeat(heights, extent[position] // parts).reshape([-1 if axis == position else 1 for axis in range(len(extent))])
    return gain


def deal_out(own_key, own, number, rows, number_of, top, limit, slope):
    sequence = jax.random.permutation(own_key, number_of)
    heavy_load, common = portions_of(number_of, rows * top, limit, slope, True), portions_of(number_of, rows * top, limit, slope, False)
    places = jnp.arange(number_of)

    def named(tallies, turn):
        used = int((tallies > 0).sum())
        fixed = max(1, used // 4)
        moved = fixed + (places - fixed + turn * (used - fixed)) % max(1, number_of - fixed)
        return jnp.zeros((number_of,), jnp.int32).at[sequence[jnp.where(places < fixed, places, moved)]].set(jnp.asarray(tallies, jnp.int32))

    tallies = jnp.where(number % 4 == 0, named(heavy_load, number // 4), named(common, number - number // 4 - 1))
    mixed = jax.random.permutation(jax.random.fold_in(own, 3), number_of)
    giver, sink = mixed[0:number_of // 2 * 2:2], mixed[1:number_of // 2 * 2:2]
    room = jnp.minimum(tallies[giver] - 1, limit - tallies[sink]) // 2
    room = jnp.where((giver == sequence[0]) | (sink == sequence[0]) | (tallies[sink] == 0), 0, jnp.maximum(room, 0))
    moved = jax.random.randint(jax.random.fold_in(own, 4), (number_of // 2,), 0, 1 << 20) % (room + 1)
    tallies = tallies.at[giver].add(-moved).at[sink].add(moved)
    items = jnp.searchsorted(jnp.cumsum(tallies), jnp.arange(rows * top), side="right").astype(jnp.int32)
    listing = items.reshape(top, rows).T
    listing = listing[jax.random.permutation(jax.random.fold_in(own, 1), rows)]
    turn = jax.random.randint(jax.random.fold_in(own, 2), (rows, 1), 0, top)
    return jnp.take_along_axis(listing, (jnp.arange(top)[None, :] + turn) % top, axis=1)


def portions_of(count, total, reach, slope, full):
    portions = [(1 << 20) // math.isqrt(rank ** slope) + 1 for rank in range(1, count + 1)]
    largest = reach if full else min(reach, max(-(-total // count), total * portions[0] // sum(portions)))
    least = 1 if total - largest >= count - 1 else 0
    given, spare = [largest] + [least] * (count - 1), total - largest - least * (count - 1)
    while spare > 0:
        candidates = [i for i in range(1, count) if given[i] < largest] or [i for i in range(1, count) if given[i] < reach]
        mass, left = sum([portions[i] for i in candidates]), spare
        for i in candidates:
            more = min(reach - given[i], max(1, left * portions[i] // mass), spare)
            given[i] = given[i] + more
            spare = spare - more
    return np.array(given)


def normal_values(key, dims, spread, bound, shards=(), held_as=jnp.bfloat16):
    level = block_levels(key, dims, shards, -0.22, 0.18) if shards else 1.0
    drawn = jax.random.normal(key, dims, jnp.float32) * spread * level
    return jnp.minimum(jnp.maximum(drawn, -bound), bound).astype(held_as)


def setup_inputs(seed: int = 0) -> dict:
    seeds = jax.random.split(jax.random.key(seed), 13)
    attn_queries = normal_values(seeds[0], (TOKENS, HEADS * HD), 1.0, 6.0, ((0, 16), (1, 8)), jnp.float32)
    attn_keys = normal_values(seeds[1], (TOKENS, HEADS * HD), 1.0, 6.0, ((0, 16), (1, 8)), jnp.float32)
    attn_values = normal_values(seeds[2], (TOKENS, HEADS * HD), 1.0, 6.0, ((0, 16), (1, 8)), jnp.float32)
    head_gain = jnp.clip(1.0 + 0.15 * jax.random.normal(seeds[3], (HD,), jnp.float32), 0.25, 1.75)
    out_weight = normal_values(seeds[4], (HEADS * HD, D), (HEADS * HD) ** -0.5, 0.09375, ((0, 8),))
    residual_in = normal_values(seeds[5], (TOKENS, D), 1.0, 6.0, ((0, 128),))
    norm_gain = jnp.clip(1.0 + 0.15 * jax.random.normal(seeds[6], (D,), jnp.float32), 0.25, 1.75)
    routed_experts_keys = jax.random.split(jax.random.fold_in(seeds[7], 1), TOKENS // ROWS_DEV)
    routed_experts_turns = jax.random.permutation(jax.random.fold_in(seeds[7], 3), TOKENS // ROWS_DEV)
    routed_experts = jax.vmap(lambda own, number: deal_out(jax.random.fold_in(seeds[7], 2), own, number, ROWS_DEV, EXPERTS, TOPK, CAP, 2))(routed_experts_keys, routed_experts_turns).reshape((TOKENS, TOPK))
    gate_weights = jnp.clip(0.05 + 0.95 * jax.random.uniform(seeds[8], (TOKENS, TOPK), jnp.float32) ** block_levels(seeds[8], (TOKENS, TOPK), ((0, 128),), -0.2, 0.2), 0.05, 1.0)
    expert_gate = normal_values(seeds[9], (EXPERTS, D, FF), D ** -0.5, 0.125, ((0, 128),))
    expert_up = normal_values(seeds[10], (EXPERTS, D, FF), D ** -0.5, 0.125, ((0, 128),))
    expert_down = normal_values(seeds[11], (EXPERTS, FF, D), FF ** -0.5, 0.21875, ((0, 128),))
    return dict(attn_queries=attn_queries, attn_keys=attn_keys, attn_values=attn_values, head_gain=head_gain, out_weight=out_weight, residual_in=residual_in, norm_gain=norm_gain, routed_experts=routed_experts, gate_weights=gate_weights, expert_gate=expert_gate, expert_up=expert_up, expert_down=expert_down)


block_rows = 128

def causal_linear(queries_here, keys_here, values_here, start_state, block_size):
    row_count = queries_here.shape[0]
    head_count = queries_here.shape[1]
    head_size = queries_here.shape[2]
    block_count = row_count // block_size
    lower_mask = jnp.tril(jnp.ones((block_size, block_size), jnp.float32))
    exact_mode = lax.Precision.HIGHEST

    def advance(state_now, inputs):
        query_block, key_block, value_block = inputs
        scores = jnp.einsum('thd,shd->hts', query_block, key_block, precision=exact_mode) * lower_mask
        within = jnp.einsum('hts,she->the', scores, value_block, precision=exact_mode)
        carried = jnp.einsum('thd,hde->the', query_block, state_now, precision=exact_mode)
        state_next = state_now + jnp.einsum('thd,the->hde', key_block, value_block, precision=exact_mode)
        return (state_next, within + carried)

    def blocked(tensor):
        return tensor.reshape(block_count, block_size, head_count, head_size)
    state_last, outputs = lax.scan(advance, start_state, (blocked(queries_here), blocked(keys_here), blocked(values_here)))
    return outputs.reshape(row_count, head_count, head_size)

def rms_scale(tensor, gain_row):
    return tensor * lax.rsqrt(lax.optimization_barrier(jnp.mean(tensor * tensor, axis=-1, keepdims=True)) + 1e-06) * gain_row

def expert_rows(moe_input, routed_experts, expert_gate, expert_up, expert_down):
    flat_experts = routed_experts.reshape(-1).astype(jnp.int32)
    total_rows = flat_experts.shape[0]
    sorted_order = jnp.argsort(flat_experts, stable=True).astype(jnp.int32)
    token_of = (sorted_order // TOPK).astype(jnp.int32)
    member = (flat_experts[:, None] == jnp.arange(EXPERTS, dtype=jnp.int32)[None, :]).astype(jnp.int32)
    counts = lax.optimization_barrier(jnp.sum(member, axis=0)).astype(jnp.int32)
    starts = (jnp.cumsum(counts) - counts).astype(jnp.int32)
    padded_tokens = jnp.concatenate([token_of, jnp.zeros((block_rows,), jnp.int32)])
    results = jnp.zeros((total_rows + block_rows, D), jnp.bfloat16)

    def per_expert(expert, results_now):
        first_row = starts[expert]
        turn_count = (counts[expert] + block_rows - 1) // block_rows

        def per_block(turn, results_in):
            offset = (first_row + turn * block_rows).astype(jnp.int32)
            tokens_here = lax.dynamic_slice_in_dim(padded_tokens, offset, block_rows)
            picked = moe_input[tokens_here]
            gate_part = jnp.dot(picked, expert_gate[expert], preferred_element_type=jnp.float32)
            up_part = jnp.dot(picked, expert_up[expert], preferred_element_type=jnp.float32)
            hidden_act = (jax.nn.silu(gate_part) * up_part).astype(jnp.bfloat16)
            produced = jnp.dot(hidden_act, expert_down[expert], preferred_element_type=jnp.float32).astype(jnp.bfloat16)
            return lax.dynamic_update_slice(results_in, produced, (offset, jnp.zeros((), jnp.int32)))
        return lax.fori_loop(0, turn_count, per_block, results_now)
    results = lax.fori_loop(0, EXPERTS, per_expert, results)
    inverse = jnp.argsort(sorted_order).astype(jnp.int32)
    return results[inverse]

def reference(attn_queries, attn_keys, attn_values, head_gain, out_weight, residual_in, norm_gain, routed_experts, gate_weights, expert_gate, expert_up, expert_down):
    block_size = min(512, TOKENS)
    start_state = jnp.zeros((HEADS, HD, HD), jnp.float32)
    attended = causal_linear(attn_queries.reshape(TOKENS, HEADS, HD), attn_keys.reshape(TOKENS, HEADS, HD), attn_values.reshape(TOKENS, HEADS, HD), start_state, block_size)
    head_normed = rms_scale(attended, head_gain).astype(jnp.bfloat16).reshape(TOKENS, HEADS * HD)
    attn_out = jnp.dot(head_normed, out_weight, preferred_element_type=jnp.float32).astype(jnp.bfloat16)
    mixed = residual_in.astype(jnp.float32) + attn_out.astype(jnp.float32)
    moe_input = rms_scale(mixed, norm_gain).astype(jnp.bfloat16)
    expert_y = expert_rows(moe_input, routed_experts, expert_gate, expert_up, expert_down)
    picked_rows = expert_y.reshape(TOKENS, TOPK, D)
    moe_out = lax.optimization_barrier(jnp.sum(gate_weights[:, :, None] * picked_rows.astype(jnp.float32), axis=1)).astype(jnp.bfloat16)
    return (attn_out, moe_out)
```

```python
import functools
import jax
import jax.numpy as jnp
from jax import lax
from jax.experimental import pallas as pl
from jax.experimental.pallas import tpu as pltpu
from jax.sharding import PartitionSpec as P

EXACT = lax.Precision.HIGHEST
F32 = jnp.float32
BF16 = jnp.bfloat16
CAP = 5
VM = pl.BlockSpec(memory_space=pltpu.VMEM)
SM = pl.BlockSpec(memory_space=pltpu.SMEM)
HB = pl.BlockSpec(memory_space=pl.ANY)
MIB = 1 << 20


def params(mib):
    return pltpu.CompilerParams(vmem_limit_bytes=mib * MIB)


def cost(flops, moved):
    return pl.CostEstimate(flops=flops, bytes_accessed=moved, transcendentals=0)


def totals_kernel(heads, hd, k_ref, v_ref, out_ref):
    for h in range(heads):
        cols = slice(h * hd, (h + 1) * hd)
        out_ref[h] = lax.dot_general(
            k_ref[:, cols], v_ref[:, cols], (((0,), (0,)), ((), ())),
            precision=EXACT, preferred_element_type=F32,
        ).astype(BF16)


def within_kernel(heads, hd, q_ref, k_ref, v_ref, out_ref):
    rows = q_ref.shape[0]
    keep = lax.broadcasted_iota(jnp.int32, (rows, rows), 0) >= lax.broadcasted_iota(
        jnp.int32, (rows, rows), 1
    )
    for h in range(heads):
        cols = slice(h * hd, (h + 1) * hd)
        scores = lax.dot_general(
            q_ref[:, cols], k_ref[:, cols], (((1,), (1,)), ((), ())),
            precision=EXACT, preferred_element_type=F32,
        )
        scores = jnp.where(keep, scores, 0.0)
        out_ref[:, cols] = jnp.dot(
            scores, v_ref[:, cols], precision=EXACT, preferred_element_type=F32
        )


def project_kernel(
    heads, hd, parts, core_ref, q_ref, in_ref, base_ref, s1_ref, s2_ref, s3_ref, gain_ref, w_ref,
    mine_ref, theirs_ref, normed_ref,
):
    rows = q_ref.shape[0]
    step = rows // parts
    core = core_ref[0]
    gain = gain_ref[...]
    for h in range(heads):
        cols = slice(h * hd, (h + 1) * hd)
        state = (
            base_ref[h] + s1_ref[h].astype(F32) + s2_ref[h].astype(F32) + s3_ref[h].astype(F32)
        )
        att = in_ref[:, cols] + jnp.dot(
            q_ref[:, cols], state, precision=EXACT, preferred_element_type=F32
        )
        mean = jnp.mean(att * att, axis=-1, keepdims=True)
        norm = (att * lax.rsqrt(mean + 1e-06) * gain).astype(BF16)
        normed_ref[:, :, cols] = norm.reshape(parts, step, hd)
    weight = w_ref[...]
    half = parts // 2

    def rows_for(which):
        return jnp.concatenate([normed_ref[2 * z + which] for z in range(half)], axis=0)

    theirs = jnp.dot(rows_for(1 - core), weight, preferred_element_type=F32)
    theirs_ref[...] = theirs.astype(BF16).reshape(theirs_ref.shape)
    mine = jnp.dot(rows_for(core), weight, preferred_element_type=F32)
    mine_ref[...] = mine.reshape(mine_ref.shape)


def pair_kernel(zs, z_ref, mine_ref, got_ref, *outs):
    z = z_ref[0]
    for k in range(zs):
        block = lax.rem(z + k, zs)
        total = mine_ref[block] + got_ref[block].astype(F32)
        outs[k][...] = total.astype(outs[k].dtype)


def routing_kernel(cap, routed_ref, slots_ref, tokens_ref):
    routed = routed_ref[...]
    top, rows = routed.shape
    experts = tokens_ref.shape[1]
    expert = lax.broadcasted_iota(jnp.int32, (experts, rows), 0)
    named = [expert == routed[k : k + 1, :] for k in range(top)]
    member = jnp.zeros((experts, rows), F32)
    for hit in named:
        member = jnp.where(hit, 1.0, member)
    earlier_token = lax.broadcasted_iota(jnp.int32, (rows, rows), 0) < lax.broadcasted_iota(
        jnp.int32, (rows, rows), 1
    )
    earlier = jnp.dot(
        member, earlier_token.astype(F32), precision=EXACT, preferred_element_type=F32
    )
    for k in range(top):
        place = jnp.sum(jnp.where(named[k], earlier, 0.0), axis=0, keepdims=True)
        slots_ref[k : k + 1, :] = place.astype(jnp.int32)
    token = lax.broadcasted_iota(jnp.int32, (8, rows), 1).astype(F32)
    for s in range(cap):
        here = jnp.where((member > 0.5) & (earlier == float(s)), 1.0, 0.0)
        found = lax.dot_general(
            token, here, (((1,), (1,)), ((), ())), precision=EXACT, preferred_element_type=F32
        )
        tokens_ref[s : s + 1, :] = found[0:1, :].astype(jnp.int32)


def dispatch_kernel(
    cap, tokens_ref, o0_ref, o1_ref, o2_ref, o3_ref, res_ref, gain_ref, attn_ref, out_ref,
    wide_ref, tile_ref,
):
    rows, width = res_ref.shape
    per = width // 128
    step = pl.program_id(0)
    group = out_ref.shape[0]

    @pl.when(step == 0)
    def _():
        total = (
            o0_ref[...] + o1_ref[...].astype(F32) + o2_ref[...].astype(F32) + o3_ref[...].astype(F32)
        )
        attn = total.astype(BF16)
        attn_ref[...] = attn
        mixed = res_ref[...].astype(F32) + attn.astype(F32)
        mean = jnp.mean(mixed * mixed, axis=-1, keepdims=True)
        normed = mixed * lax.rsqrt(mean + 1e-06) * gain_ref[...]
        for j in range(per):
            wide_ref[pl.ds(j, rows, stride=per), :] = normed[:, j * 128 : (j + 1) * 128]
        tile_ref[...] = wide_ref[...].astype(BF16).reshape(rows, per, 128)

    for d in range(group):
        for s in range(cap):
            token = tokens_ref[s, step * group + d]
            out_ref[d, :, s * 128 : (s + 1) * 128] = tile_ref[token]


def expert_kernel(
    cap, in_hbm, gate_hbm, up_hbm, down_hbm, out_hbm,
    got, rows_ref, gate_ref, up_ref, down_ref, act_ref, turned, back,
    in_sem, gate_sem, up_sem, down_sem, out_sem,
):
    peers, per, _ = got.shape
    groups = peers // 16
    span = per * 16
    width = rows_ref.shape[1]
    hidden = act_ref.shape[1]
    tile = 256

    in_copies = [
        pltpu.make_async_copy(
            in_hbm.at[pl.ds(g * 16, 16)], got.at[pl.ds(g * 16, 16)], in_sem.at[g]
        )
        for g in range(groups)
    ]
    for copy in in_copies:
        copy.start()
    gate_copies, up_copies = [], []
    for n in range(hidden // tile):
        cols = pl.ds(n * tile, tile)
        gate_copies.append(
            pltpu.make_async_copy(gate_hbm.at[0, :, cols], gate_ref.at[:, cols], gate_sem.at[n])
        )
        up_copies.append(
            pltpu.make_async_copy(up_hbm.at[0, :, cols], up_ref.at[:, cols], up_sem.at[n])
        )
        gate_copies[-1].start()
        up_copies[-1].start()
    down_copies = []
    for n in range(width // 1024):
        cols = pl.ds(n * 1024, 1024)
        down_copies.append(
            pltpu.make_async_copy(down_hbm.at[0, :, cols], down_ref.at[:, cols], down_sem.at[n])
        )
        down_copies[-1].start()

    to = lax.broadcasted_iota(jnp.int32, (span, span), 0)
    fro = lax.broadcasted_iota(jnp.int32, (span, span), 1)
    swap = (fro == (to & 15) * 16 + (to >> 4)).astype(BF16)

    for g in range(groups):
        in_copies[g].wait()
        flat = got[g * 16 : (g + 1) * 16].reshape(span, cap * 128)
        moved = jnp.dot(swap, flat, preferred_element_type=F32).astype(BF16)
        for j in range(per):
            for s in range(cap):
                rows_ref[s * peers + g * 16 : s * peers + g * 16 + 16, j * 128 : (j + 1) * 128] = (
                    moved[j * 16 : (j + 1) * 16, s * 128 : (s + 1) * 128]
                )

    for n in range(hidden // tile):
        cols = slice(n * tile, (n + 1) * tile)
        gate_copies[n].wait()
        gate = jnp.dot(rows_ref[...], gate_ref[:, cols], preferred_element_type=F32)
        up_copies[n].wait()
        up = jnp.dot(rows_ref[...], up_ref[:, cols], preferred_element_type=F32)
        act_ref[:, cols] = (gate / (1.0 + jnp.exp(-gate)) * up).astype(BF16)

    for n in range(width // tile):
        if n % (1024 // tile) == 0:
            down_copies[n // (1024 // tile)].wait()
        made = jnp.dot(
            act_ref[...], down_ref[:, n * tile : (n + 1) * tile], preferred_element_type=F32
        ).astype(BF16)
        for jj in range(tile // 128):
            j = n * (tile // 128) + jj
            for g in range(groups):
                for s in range(cap):
                    turned[g, j * 16 : (j + 1) * 16, s * 128 : (s + 1) * 128] = made[
                        s * peers + g * 16 : s * peers + g * 16 + 16, jj * 128 : (jj + 1) * 128
                    ]

    out_copies = []
    for g in range(groups):
        back[g * 16 : (g + 1) * 16] = (
            jnp.dot(swap, turned[g], preferred_element_type=F32)
            .astype(BF16)
            .reshape(16, per, cap * 128)
        )
        out_copies.append(
            pltpu.make_async_copy(
                back.at[pl.ds(g * 16, 16)], out_hbm.at[pl.ds(g * 16, 16)], out_sem.at[g]
            )
        )
        out_copies[-1].start()
    for copy in out_copies:
        copy.wait()


def combine_kernel(routed_ref, slots_ref, weights_ref, back_ref, out_ref, wide_ref):
    top, rows = routed_ref.shape
    per = back_ref.shape[1]
    for t in range(rows):
        total = jnp.zeros((per, 128), F32)
        for k in range(top):
            slot = pl.multiple_of(slots_ref[k, t] * 128, 128)
            tile = back_ref[routed_ref[k, t], :, pl.ds(slot, 128)]
            total = total + weights_ref[k, t] * tile.astype(F32)
        wide_ref[t * per : (t + 1) * per, :] = total
    for j in range(per):
        out_ref[:, j * 128 : (j + 1) * 128] = wide_ref[pl.ds(j, rows, stride=per), :].astype(
            out_ref.dtype
        )


def shards(
    ys,
    attn_queries,
    attn_keys,
    attn_values,
    head_gain,
    out_weight,
    residual_in,
    norm_gain,
    routed_experts,
    gate_weights,
    expert_gate,
    expert_up,
    expert_down,
):
    rows, local = attn_queries.shape
    hd = head_gain.shape[0]
    heads = local // hd
    width = out_weight.shape[1]
    seqs = lax.axis_size("seq")
    parts = lax.axis_size("head")
    xs, zs = seqs // ys, parts // 2
    peers = seqs * parts
    hidden = expert_gate.shape[2]
    own_rows, top = routed_experts.shape
    per = width // 128
    cap = CAP
    y = lax.rem(lax.axis_index("seq"), ys)
    head = lax.axis_index("head")
    core = lax.rem(head, 2).reshape(1)
    z = (head // 2).reshape(1)

    state_shape = (heads, hd, hd)
    totals = pl.pallas_call(
        functools.partial(totals_kernel, heads, hd),
        out_shape=jax.ShapeDtypeStruct(state_shape, BF16),
        in_specs=[VM] * 2,
        out_specs=VM,
        compiler_params=params(16),
        name="totals",
    )(attn_keys, attn_values)

    from_y = [
        lax.ppermute(
            totals, "seq", [(i, (i // ys) * ys + (i + k) % ys) for i in range(seqs)]
        )
        for k in range(1, ys)
    ]
    within = pl.pallas_call(
        functools.partial(within_kernel, heads, hd),
        out_shape=jax.ShapeDtypeStruct((rows, local), F32),
        in_specs=[VM] * 3,
        out_specs=VM,
        compiler_params=params(24),
        cost_estimate=cost(12 * heads * rows * rows * hd * 2, 16 * rows * local),
        name="within",
    )(attn_queries, attn_keys, attn_values)
    routed = routed_experts.T
    slots, tokens = pl.pallas_call(
        functools.partial(routing_kernel, cap),
        out_shape=(
            jax.ShapeDtypeStruct((top, own_rows), jnp.int32),
            jax.ShapeDtypeStruct((8, peers), jnp.int32),
        ),
        in_specs=[VM],
        out_specs=(VM, VM),
        compiler_params=params(8),
        name="routing",
    )(routed)

    plane = totals.astype(F32)
    base = jnp.zeros(state_shape, F32)
    for k, part in enumerate(from_y, 1):
        wide = part.astype(F32)
        plane = plane + wide
        base = base + jnp.where(y >= k, wide, 0.0)
    plane = plane.astype(BF16)
    from_x = [
        lax.ppermute(plane, "seq", [(i, i + k * ys) for i in range(seqs - k * ys)])
        for k in range(1, xs)
    ]

    mine, theirs = pl.pallas_call(
        functools.partial(project_kernel, heads, hd, parts),
        out_shape=(
            jax.ShapeDtypeStruct((zs, own_rows, width), F32),
            jax.ShapeDtypeStruct((zs, own_rows, width), BF16),
        ),
        in_specs=[SM] + [VM] * 8,
        out_specs=(VM, VM),
        scratch_shapes=[pltpu.VMEM((parts, own_rows, local), BF16)],
        compiler_params=params(32),
        name="project",
    )(
        core, attn_queries, within, base, *from_x, head_gain.reshape(1, hd), out_weight
    )
    got = lax.ppermute(theirs, "head", [(i, i ^ 1) for i in range(parts)])
    blocks = pl.pallas_call(
        functools.partial(pair_kernel, zs),
        out_shape=tuple(
            jax.ShapeDtypeStruct((own_rows, width), F32 if k == 0 else BF16) for k in range(zs)
        ),
        in_specs=[SM, VM, VM],
        out_specs=(VM,) * zs,
        compiler_params=params(16),
        name="pair",
    )(z, mine, got)
    from_z = [
        lax.ppermute(blocks[k], "head", [(i, (i + 2 * k) % parts) for i in range(parts)])
        for k in range(1, zs)
    ]

    groups = 4
    whole = pl.BlockSpec((own_rows, width), lambda i: (0, 0))
    attn_out, outgoing = pl.pallas_call(
        functools.partial(dispatch_kernel, cap),
        out_shape=(
            jax.ShapeDtypeStruct((own_rows, width), BF16),
            jax.ShapeDtypeStruct((peers, per, cap * 128), BF16),
        ),
        grid=(groups,),
        in_specs=[SM] + [whole] * 5 + [pl.BlockSpec((1, width), lambda i: (0, 0))],
        out_specs=(whole, pl.BlockSpec((peers // groups, per, cap * 128), lambda i: (i, 0, 0))),
        scratch_shapes=[
            pltpu.VMEM((own_rows * per, 128), F32),
            pltpu.VMEM((own_rows, per, 128), BF16),
        ],
        compiler_params=params(16),
        name="dispatch",
    )(tokens, blocks[0], *from_z, residual_in, norm_gain.reshape(1, width))

    arrived = lax.all_to_all(outgoing, ("seq", "head"), split_axis=0, concat_axis=0, tiled=True)

    groups16 = peers // 16
    produced = pl.pallas_call(
        functools.partial(expert_kernel, cap),
        out_shape=jax.ShapeDtypeStruct((peers, per, cap * 128), BF16),
        in_specs=[HB] * 4,
        out_specs=HB,
        scratch_shapes=[
            pltpu.VMEM((peers, per, cap * 128), BF16),
            pltpu.VMEM((cap * peers, width), BF16),
            pltpu.VMEM((width, hidden), BF16),
            pltpu.VMEM((width, hidden), BF16),
            pltpu.VMEM((hidden, width), BF16),
            pltpu.VMEM((cap * peers, hidden), BF16),
            pltpu.VMEM((groups16, per * 16, cap * 128), BF16),
            pltpu.VMEM((peers, per, cap * 128), BF16),
            pltpu.SemaphoreType.DMA((groups16,)),
            pltpu.SemaphoreType.DMA((hidden // 256,)),
            pltpu.SemaphoreType.DMA((hidden // 256,)),
            pltpu.SemaphoreType.DMA((width // 1024,)),
            pltpu.SemaphoreType.DMA((groups16,)),
        ],
        compiler_params=params(48),
        name="expert",
    )(arrived, expert_gate, expert_up, expert_down)

    returned = lax.all_to_all(produced, ("seq", "head"), split_axis=0, concat_axis=0, tiled=True)

    moe_out = pl.pallas_call(
        combine_kernel,
        out_shape=jax.ShapeDtypeStruct((own_rows, width), BF16),
        in_specs=[SM, SM, SM, VM],
        out_specs=VM,
        scratch_shapes=[pltpu.VMEM((own_rows * per, 128), F32)],
        compiler_params=params(16),
        name="combine",
    )(routed, slots, gate_weights.T, returned)
    return (attn_out, moe_out)


def solution(mesh):
    return jax.shard_map(
        functools.partial(shards, 4),
        mesh=mesh,
        in_specs=(
            P("seq", "head"),
            P("seq", "head"),
            P("seq", "head"),
            P(),
            P("head", None),
            P(("seq", "head"), None),
            P(),
            P(("seq", "head"), None),
            P(("seq", "head"), None),
            P(("seq", "head"), None, None),
            P(("seq", "head"), None, None),
            P(("seq", "head"), None, None),
        ),
        out_specs=(P(("seq", "head"), None), P(("seq", "head"), None)),
        check_vma=False,
    )
```

```python
import functools
import jax
import jax.numpy as jnp
from jax import lax
from jax.experimental import pallas as pl
from jax.experimental.pallas import tpu as pltpu
from jax.sharding import PartitionSpec as P

EXACT = lax.Precision.HIGHEST
F32 = jnp.float32
BF16 = jnp.bfloat16
CAP = 5
VM = pl.BlockSpec(memory_space=pltpu.VMEM)
SM = pl.BlockSpec(memory_space=pltpu.SMEM)
HB = pl.BlockSpec(memory_space=pltpu.HBM)
MIB = 1 << 20


def in_hbm(array):
    return pltpu.with_memory_space_constraint(array, pltpu.HBM)


def params(mib):
    return pltpu.CompilerParams(vmem_limit_bytes=mib * MIB)


def cost(flops, moved):
    return pl.CostEstimate(flops=flops, bytes_accessed=moved, transcendentals=0)


def totals_kernel(heads, hd, q_hbm, k_hbm, v_hbm, out_ref, q_ref, k_ref, v_ref, sems):
    copies = [
        pltpu.make_async_copy(src, dst, sems.at[n])
        for n, (src, dst) in enumerate([(k_hbm, k_ref), (v_hbm, v_ref), (q_hbm, q_ref)])
    ]
    for copy in copies:
        copy.start()
    copies[0].wait()
    copies[1].wait()
    for h in range(heads):
        cols = slice(h * hd, (h + 1) * hd)
        out_ref[h] = lax.dot_general(
            k_ref[:, cols], v_ref[:, cols], (((0,), (0,)), ((), ())),
            precision=EXACT, preferred_element_type=F32,
        ).astype(BF16)
    copies[2].wait()


def within_kernel(heads, hd, q_ref, k_ref, v_ref, out_ref):
    rows = q_ref.shape[0]
    keep = lax.broadcasted_iota(jnp.int32, (rows, rows), 0) >= lax.broadcasted_iota(
        jnp.int32, (rows, rows), 1
    )
    for h in range(heads):
        cols = slice(h * hd, (h + 1) * hd)
        scores = lax.dot_general(
            q_ref[:, cols], k_ref[:, cols], (((1,), (1,)), ((), ())),
            precision=EXACT, preferred_element_type=F32,
        )
        scores = jnp.where(keep, scores, 0.0)
        out_ref[:, cols] = jnp.dot(
            scores, v_ref[:, cols], precision=EXACT, preferred_element_type=F32
        )


def plane_kernel(own_ref, *refs):
    parts, plane_ref, base_ref = refs[:-3], refs[-2], refs[-1]
    y = lax.rem(lax.axis_index("seq"), len(parts) + 1)
    plane = own_ref[...].astype(F32)
    base = jnp.zeros(own_ref.shape, F32)
    for k, part in enumerate(parts, 1):
        wide = part[...].astype(F32)
        plane = plane + wide
        base = base + jnp.where(y >= k, wide, 0.0)
    plane_ref[...] = plane.astype(BF16)
    base_ref[...] = base


def project_kernel(
    heads, hd, parts, q_ref, in_ref, base_ref, s1_ref, s2_ref, s3_ref, gain_ref, w_ref,
    normed_ref, theirs_ref,
):
    rows = q_ref.shape[0]
    step = rows // parts
    core = lax.rem(lax.axis_index("head"), 2)
    gain = gain_ref[...]
    for h in range(heads):
        cols = slice(h * hd, (h + 1) * hd)
        state = (
            base_ref[h] + s1_ref[h].astype(F32) + s2_ref[h].astype(F32) + s3_ref[h].astype(F32)
        )
        att = in_ref[:, cols] + jnp.dot(
            q_ref[:, cols], state, precision=EXACT, preferred_element_type=F32
        )
        mean = jnp.mean(att * att, axis=-1, keepdims=True)
        norm = (att * lax.rsqrt(mean + 1e-06) * gain).astype(BF16)
        normed_ref[:, :, cols] = norm.reshape(parts, step, hd)
    theirs_ref[...] = projected(normed_ref, w_ref, 1 - core).astype(BF16)


def projected(normed_ref, w_ref, which):
    half = normed_ref.shape[0] // 2
    picked = jnp.concatenate([normed_ref[2 * z + which] for z in range(half)], axis=0)
    made = jnp.dot(picked, w_ref[...], preferred_element_type=F32)
    return made.reshape(half, normed_ref.shape[1], w_ref.shape[1])


def keep_kernel(normed_ref, w_ref, mine_ref):
    mine_ref[...] = projected(normed_ref, w_ref, lax.rem(lax.axis_index("head"), 2))


def pair_kernel(zs, mine_ref, got_ref, *outs):
    z = lax.div(lax.axis_index("head"), 2)
    for k in range(zs):
        block = lax.rem(z + k, zs)
        total = mine_ref[block] + got_ref[block].astype(F32)
        outs[k][...] = total.astype(outs[k].dtype)


def routing_kernel(cap, routed_ref, slots_ref, tokens_ref):
    routed = routed_ref[...]
    top, rows = routed.shape
    experts = tokens_ref.shape[1]
    expert = lax.broadcasted_iota(jnp.int32, (experts, rows), 0)
    named = [expert == routed[k : k + 1, :] for k in range(top)]
    member = jnp.zeros((experts, rows), F32)
    for hit in named:
        member = jnp.where(hit, 1.0, member)
    earlier_token = lax.broadcasted_iota(jnp.int32, (rows, rows), 0) < lax.broadcasted_iota(
        jnp.int32, (rows, rows), 1
    )
    earlier = jnp.dot(
        member, earlier_token.astype(F32), precision=EXACT, preferred_element_type=F32
    )
    for k in range(top):
        place = jnp.sum(jnp.where(named[k], earlier, 0.0), axis=0, keepdims=True)
        slots_ref[k : k + 1, :] = place.astype(jnp.int32)
    token = lax.broadcasted_iota(jnp.int32, (8, rows), 1).astype(F32)
    for s in range(cap):
        here = jnp.where((member > 0.5) & (earlier == float(s)), 1.0, 0.0)
        found = lax.dot_general(
            token, here, (((1,), (1,)), ((), ())), precision=EXACT, preferred_element_type=F32
        )
        tokens_ref[s : s + 1, :] = found[0:1, :].astype(jnp.int32)


def dispatch_kernel(
    cap, tokens_ref, o0_ref, o1_ref, o2_ref, o3_ref, res_ref, gain_ref, attn_ref, out_ref,
    wide_ref, tile_ref,
):
    rows, width = res_ref.shape
    per = width // 128
    total = (
        o0_ref[...] + o1_ref[...].astype(F32) + o2_ref[...].astype(F32) + o3_ref[...].astype(F32)
    )
    attn = total.astype(BF16)
    attn_ref[...] = attn
    mixed = res_ref[...].astype(F32) + attn.astype(F32)
    mean = jnp.mean(mixed * mixed, axis=-1, keepdims=True)
    normed = mixed * lax.rsqrt(mean + 1e-06) * gain_ref[...]
    for j in range(per):
        wide_ref[pl.ds(j, rows, stride=per), :] = normed[:, j * 128 : (j + 1) * 128]
    tile_ref[...] = wide_ref[...].astype(BF16).reshape(rows, per, 128)

    for d in range(out_ref.shape[0]):
        for s in range(cap):
            out_ref[d, :, s * 128 : (s + 1) * 128] = tile_ref[tokens_ref[s, d]]


def expert_kernel(
    cap, in_ref, gate_ref, up_ref, down_ref, out_ref, rows_ref, act_ref, turned
):
    peers, per, _ = in_ref.shape
    groups = peers // 16
    span = per * 16
    width = rows_ref.shape[1]
    hidden = act_ref.shape[1]
    tile = 256

    to = lax.broadcasted_iota(jnp.int32, (span, span), 0)
    fro = lax.broadcasted_iota(jnp.int32, (span, span), 1)
    swap = (fro == (to & 15) * 16 + (to >> 4)).astype(BF16)

    for g in range(groups):
        flat = in_ref[g * 16 : (g + 1) * 16].reshape(span, cap * 128)
        moved = jnp.dot(swap, flat, preferred_element_type=F32).astype(BF16)
        for j in range(per):
            for s in range(cap):
                rows_ref[s * peers + g * 16 : s * peers + g * 16 + 16, j * 128 : (j + 1) * 128] = (
                    moved[j * 16 : (j + 1) * 16, s * 128 : (s + 1) * 128]
                )

    for n in range(hidden // tile):
        cols = slice(n * tile, (n + 1) * tile)
        gate = jnp.dot(rows_ref[...], gate_ref[0, :, cols], preferred_element_type=F32)
        up = jnp.dot(rows_ref[...], up_ref[0, :, cols], preferred_element_type=F32)
        act_ref[:, cols] = (gate / (1.0 + jnp.exp(-gate)) * up).astype(BF16)

    for n in range(width // tile):
        made = jnp.dot(
            act_ref[...], down_ref[0, :, n * tile : (n + 1) * tile], preferred_element_type=F32
        ).astype(BF16)
        for jj in range(tile // 128):
            j = n * (tile // 128) + jj
            for g in range(groups):
                for s in range(cap):
                    turned[g, j * 16 : (j + 1) * 16, s * 128 : (s + 1) * 128] = made[
                        s * peers + g * 16 : s * peers + g * 16 + 16, jj * 128 : (jj + 1) * 128
                    ]

    for g in range(groups):
        out_ref[g * 16 : (g + 1) * 16] = (
            jnp.dot(swap, turned[g], preferred_element_type=F32)
            .astype(BF16)
            .reshape(16, per, cap * 128)
        )


def combine_kernel(routed_ref, slots_ref, weights_ref, back_ref, out_ref, wide_ref):
    top, rows = routed_ref.shape
    per = back_ref.shape[1]
    for t in range(rows):
        total = jnp.zeros((per, 128), F32)
        for k in range(top):
            slot = pl.multiple_of(slots_ref[k, t] * 128, 128)
            tile = back_ref[routed_ref[k, t], :, pl.ds(slot, 128)]
            total = total + weights_ref[k, t] * tile.astype(F32)
        wide_ref[t * per : (t + 1) * per, :] = total
    for j in range(per):
        out_ref[:, j * 128 : (j + 1) * 128] = wide_ref[pl.ds(j, rows, stride=per), :].astype(
            out_ref.dtype
        )


def shards(
    ys,
    attn_queries,
    attn_keys,
    attn_values,
    head_gain,
    out_weight,
    residual_in,
    norm_gain,
    routed_experts,
    gate_weights,
    expert_gate,
    expert_up,
    expert_down,
):
    rows, local = attn_queries.shape
    hd = head_gain.shape[0]
    heads = local // hd
    width = out_weight.shape[1]
    seqs = lax.axis_size("seq")
    parts = lax.axis_size("head")
    xs, zs = seqs // ys, parts // 2
    peers = seqs * parts
    hidden = expert_gate.shape[2]
    own_rows, top = routed_experts.shape
    per = width // 128
    cap = CAP

    state_shape = (heads, hd, hd)
    totals, queries, keys, values = pl.pallas_call(
        functools.partial(totals_kernel, heads, hd),
        out_shape=(jax.ShapeDtypeStruct(state_shape, BF16),)
        + (jax.ShapeDtypeStruct((rows, local), F32),) * 3,
        in_specs=[HB] * 3,
        out_specs=(VM,) * 4,
        scratch_shapes=[pltpu.SemaphoreType.DMA((3,))],
        compiler_params=params(2),
        name="totals",
    )(*(in_hbm(part) for part in (attn_queries, attn_keys, attn_values)))

    from_y = [
        lax.ppermute(
            totals, "seq", [(i, (i // ys) * ys + (i + k) % ys) for i in range(seqs)]
        )
        for k in range(1, ys)
    ]
    within = pl.pallas_call(
        functools.partial(within_kernel, heads, hd),
        out_shape=jax.ShapeDtypeStruct((rows, local), F32),
        in_specs=[VM] * 3,
        out_specs=VM,
        compiler_params=params(2),
        cost_estimate=cost(12 * heads * rows * rows * hd * 2, 16 * rows * local),
        name="within",
    )(queries, keys, values)
    routed = routed_experts.T
    slots, tokens = pl.pallas_call(
        functools.partial(routing_kernel, cap),
        out_shape=(
            jax.ShapeDtypeStruct((top, own_rows), jnp.int32),
            jax.ShapeDtypeStruct((8, peers), jnp.int32),
        ),
        in_specs=[VM],
        out_specs=(VM, VM),
        compiler_params=params(2),
        name="routing",
    )(routed)

    plane, base = pl.pallas_call(
        plane_kernel,
        out_shape=(
            jax.ShapeDtypeStruct(state_shape, BF16),
            jax.ShapeDtypeStruct(state_shape, F32),
        ),
        in_specs=[VM] * ys + [pl.BlockSpec(memory_space=pl.ANY)],
        out_specs=(VM, VM),
        compiler_params=params(2),
        name="plane",
    )(totals, *from_y, within)
    from_x = [
        lax.ppermute(plane, "seq", [(i, i + k * ys) for i in range(seqs - k * ys)])
        for k in range(1, xs)
    ]

    normed, theirs = pl.pallas_call(
        functools.partial(project_kernel, heads, hd, parts),
        out_shape=(
            jax.ShapeDtypeStruct((parts, own_rows, local), BF16),
            jax.ShapeDtypeStruct((zs, own_rows, width), BF16),
        ),
        in_specs=[VM] * 8,
        out_specs=(VM, VM),
        compiler_params=params(2),
        name="project",
    )(
        queries, within, base, *from_x, head_gain.reshape(1, hd), out_weight
    )
    got = lax.ppermute(theirs, "head", [(i, i ^ 1) for i in range(parts)])
    mine = pl.pallas_call(
        keep_kernel,
        out_shape=jax.ShapeDtypeStruct((zs, own_rows, width), F32),
        in_specs=[VM, VM],
        out_specs=VM,
        compiler_params=params(2),
        name="keep",
    )(normed, out_weight)
    blocks = pl.pallas_call(
        functools.partial(pair_kernel, zs),
        out_shape=tuple(
            jax.ShapeDtypeStruct((own_rows, width), F32 if k == 0 else BF16) for k in range(zs)
        ),
        in_specs=[VM, VM],
        out_specs=(VM,) * zs,
        compiler_params=params(2),
        name="pair",
    )(mine, got)
    from_z = [
        lax.ppermute(blocks[k], "head", [(i, (i + 2 * k) % parts) for i in range(parts)])
        for k in range(1, zs)
    ]

    attn_out, outgoing = pl.pallas_call(
        functools.partial(dispatch_kernel, cap),
        out_shape=(
            jax.ShapeDtypeStruct((own_rows, width), BF16),
            jax.ShapeDtypeStruct((peers, per, cap * 128), BF16),
        ),
        in_specs=[SM] + [VM] * 6,
        out_specs=(VM, VM),
        scratch_shapes=[
            pltpu.VMEM((own_rows * per, 128), F32),
            pltpu.VMEM((own_rows, per, 128), BF16),
        ],
        compiler_params=params(2),
        name="dispatch",
    )(tokens, blocks[0], *from_z, residual_in, norm_gain.reshape(1, width))

    arrived = lax.all_to_all(outgoing, ("seq", "head"), split_axis=0, concat_axis=0, tiled=True)

    produced = pl.pallas_call(
        functools.partial(expert_kernel, cap),
        out_shape=jax.ShapeDtypeStruct((peers, per, cap * 128), BF16),
        in_specs=[VM] * 4,
        out_specs=VM,
        scratch_shapes=[
            pltpu.VMEM((cap * peers, width), BF16),
            pltpu.VMEM((cap * peers, hidden), BF16),
            pltpu.VMEM((peers // 16, per * 16, cap * 128), BF16),
        ],
        compiler_params=params(8),
        name="expert",
    )(arrived, expert_gate, expert_up, expert_down)

    returned = lax.all_to_all(produced, ("seq", "head"), split_axis=0, concat_axis=0, tiled=True)

    moe_out = pl.pallas_call(
        combine_kernel,
        out_shape=jax.ShapeDtypeStruct((own_rows, width), BF16),
        in_specs=[SM, SM, SM, VM],
        out_specs=VM,
        scratch_shapes=[pltpu.VMEM((own_rows * per, 128), F32)],
        compiler_params=params(2),
        name="combine",
    )(routed, slots, gate_weights.T, returned)
    return (attn_out, moe_out)


def solution(mesh):
    return jax.shard_map(
        functools.partial(shards, 4),
        mesh=mesh,
        in_specs=(
            P("seq", "head"),
            P("seq", "head"),
            P("seq", "head"),
            P(),
            P("head", None),
            P(("seq", "head"), None),
            P(),
            P(("seq", "head"), None),
            P(("seq", "head"), None),
            P(("seq", "head"), None, None),
            P(("seq", "head"), None, None),
            P(("seq", "head"), None, None),
        ),
        out_specs=(P(("seq", "head"), None), P(("seq", "head"), None)),
        check_vma=False,
    )
```

```python
import functools
import jax
import jax.numpy as jnp
from jax import lax
from jax.experimental import pallas as pl
from jax.experimental.pallas import tpu as pltpu
from jax.sharding import PartitionSpec as P

EXACT = lax.Precision.HIGHEST
F32 = jnp.float32
BF16 = jnp.bfloat16
CAP = 5
VM = pl.BlockSpec(memory_space=pltpu.VMEM)
SM = pl.BlockSpec(memory_space=pltpu.SMEM)
HB = pl.BlockSpec(memory_space=pltpu.HBM)
MIB = 1 << 20


def in_hbm(array):
    return pltpu.with_memory_space_constraint(array, pltpu.HBM)


def params(mib):
    return pltpu.CompilerParams(vmem_limit_bytes=mib * MIB)


def cost(flops, moved):
    return pl.CostEstimate(flops=flops, bytes_accessed=moved, transcendentals=0)


def totals_kernel(heads, hd, q_hbm, k_hbm, v_hbm, out_ref, q_ref, k_ref, v_ref, sems):
    copies = [
        pltpu.make_async_copy(src, dst, sems.at[n])
        for n, (src, dst) in enumerate([(k_hbm, k_ref), (v_hbm, v_ref), (q_hbm, q_ref)])
    ]
    for copy in copies:
        copy.start()
    copies[0].wait()
    copies[1].wait()
    for h in range(heads):
        cols = slice(h * hd, (h + 1) * hd)
        out_ref[h] = lax.dot_general(
            k_ref[:, cols], v_ref[:, cols], (((0,), (0,)), ((), ())),
            precision=EXACT, preferred_element_type=F32,
        ).astype(BF16)
    copies[2].wait()


def within_kernel(heads, hd, q_ref, k_ref, v_ref, out_ref):
    rows = q_ref.shape[0]
    keep = lax.broadcasted_iota(jnp.int32, (rows, rows), 0) >= lax.broadcasted_iota(
        jnp.int32, (rows, rows), 1
    )
    for h in range(heads):
        cols = slice(h * hd, (h + 1) * hd)
        scores = lax.dot_general(
            q_ref[:, cols], k_ref[:, cols], (((1,), (1,)), ((), ())),
            precision=EXACT, preferred_element_type=F32,
        )
        scores = jnp.where(keep, scores, 0.0)
        out_ref[:, cols] = jnp.dot(
            scores, v_ref[:, cols], precision=EXACT, preferred_element_type=F32
        )


def plane_kernel(own_ref, *refs):
    parts, plane_ref, base_ref = refs[:-3], refs[-2], refs[-1]
    y = lax.rem(lax.axis_index("seq"), len(parts) + 1)
    plane = own_ref[...].astype(F32)
    base = jnp.zeros(own_ref.shape, F32)
    for k, part in enumerate(parts, 1):
        wide = part[...].astype(F32)
        plane = plane + wide
        base = base + jnp.where((y ^ k) < y, wide, 0.0)
    plane_ref[...] = plane.astype(BF16)
    base_ref[...] = base


def project_kernel(
    heads, hd, parts, ys, q_ref, in_ref, base_ref, s1_ref, s2_ref, s3_ref, gain_ref, w_ref,
    normed_ref, theirs_ref,
):
    rows = q_ref.shape[0]
    step = rows // parts
    core = lax.rem(lax.axis_index("head"), 2)
    x = lax.div(lax.axis_index("seq"), ys)
    gain = gain_ref[...]
    for h in range(heads):
        cols = slice(h * hd, (h + 1) * hd)
        state = base_ref[h]
        for k, part in enumerate((s1_ref, s2_ref, s3_ref), 1):
            state = state + jnp.where((x ^ k) < x, part[h].astype(F32), 0.0)
        att = in_ref[:, cols] + jnp.dot(
            q_ref[:, cols], state, precision=EXACT, preferred_element_type=F32
        )
        mean = jnp.mean(att * att, axis=-1, keepdims=True)
        norm = (att * lax.rsqrt(mean + 1e-06) * gain).astype(BF16)
        normed_ref[:, :, cols] = norm.reshape(parts, step, hd)
    theirs_ref[...] = projected(normed_ref, w_ref, 1 - core).astype(BF16)


def projected(normed_ref, w_ref, which):
    half = normed_ref.shape[0] // 2
    picked = jnp.concatenate([normed_ref[2 * z + which] for z in range(half)], axis=0)
    made = jnp.dot(picked, w_ref[...], preferred_element_type=F32)
    return made.reshape(half, normed_ref.shape[1], w_ref.shape[1])


def keep_kernel(normed_ref, w_ref, mine_ref):
    mine_ref[...] = projected(normed_ref, w_ref, lax.rem(lax.axis_index("head"), 2))


def pair_kernel(zs, mine_ref, got_ref, *outs):
    z = lax.div(lax.axis_index("head"), 2)
    for k in range(zs):
        block = z ^ k
        total = mine_ref[block] + got_ref[block].astype(F32)
        outs[k][...] = total.astype(outs[k].dtype)


def routing_kernel(cap, routed_ref, slots_ref, tokens_ref):
    routed = routed_ref[...]
    top, rows = routed.shape
    experts = tokens_ref.shape[1]
    expert = lax.broadcasted_iota(jnp.int32, (experts, rows), 0)
    named = [expert == routed[k : k + 1, :] for k in range(top)]
    member = jnp.zeros((experts, rows), F32)
    for hit in named:
        member = jnp.where(hit, 1.0, member)
    earlier_token = lax.broadcasted_iota(jnp.int32, (rows, rows), 0) < lax.broadcasted_iota(
        jnp.int32, (rows, rows), 1
    )
    earlier = jnp.dot(
        member, earlier_token.astype(F32), precision=EXACT, preferred_element_type=F32
    )
    for k in range(top):
        place = jnp.sum(jnp.where(named[k], earlier, 0.0), axis=0, keepdims=True)
        slots_ref[k : k + 1, :] = place.astype(jnp.int32)
    token = lax.broadcasted_iota(jnp.int32, (8, rows), 1).astype(F32)
    for s in range(cap):
        here = jnp.where((member > 0.5) & (earlier == float(s)), 1.0, 0.0)
        found = lax.dot_general(
            token, here, (((1,), (1,)), ((), ())), precision=EXACT, preferred_element_type=F32
        )
        tokens_ref[s : s + 1, :] = found[0:1, :].astype(jnp.int32)


def dispatch_kernel(
    cap, tokens_ref, o0_ref, o1_ref, o2_ref, o3_ref, res_ref, gain_ref, attn_ref, out_ref,
    wide_ref, tile_ref,
):
    rows, width = res_ref.shape
    per = width // 128
    total = (
        o0_ref[...] + o1_ref[...].astype(F32) + o2_ref[...].astype(F32) + o3_ref[...].astype(F32)
    )
    attn = total.astype(BF16)
    attn_ref[...] = attn
    mixed = res_ref[...].astype(F32) + attn.astype(F32)
    mean = jnp.mean(mixed * mixed, axis=-1, keepdims=True)
    normed = mixed * lax.rsqrt(mean + 1e-06) * gain_ref[...]
    for j in range(per):
        wide_ref[pl.ds(j, rows, stride=per), :] = normed[:, j * 128 : (j + 1) * 128]
    tile_ref[...] = wide_ref[...].astype(BF16).reshape(rows, per, 128)

    for d in range(out_ref.shape[0]):
        for s in range(cap):
            out_ref[d, :, s * 128 : (s + 1) * 128] = tile_ref[tokens_ref[s, d]]


def expert_kernel(
    cap, in_ref, gate_ref, up_ref, down_ref, out_ref, rows_ref, act_ref, turned
):
    peers, per, _ = in_ref.shape
    groups = peers // 16
    span = per * 16
    width = rows_ref.shape[1]
    hidden = act_ref.shape[1]
    tile = 256

    to = lax.broadcasted_iota(jnp.int32, (span, span), 0)
    fro = lax.broadcasted_iota(jnp.int32, (span, span), 1)
    swap = (fro == (to & 15) * 16 + (to >> 4)).astype(BF16)

    for g in range(groups):
        flat = in_ref[g * 16 : (g + 1) * 16].reshape(span, cap * 128)
        moved = jnp.dot(swap, flat, preferred_element_type=F32).astype(BF16)
        for j in range(per):
            for s in range(cap):
                rows_ref[s * peers + g * 16 : s * peers + g * 16 + 16, j * 128 : (j + 1) * 128] = (
                    moved[j * 16 : (j + 1) * 16, s * 128 : (s + 1) * 128]
                )

    for n in range(hidden // tile):
        cols = slice(n * tile, (n + 1) * tile)
        gate = jnp.dot(rows_ref[...], gate_ref[0, :, cols], preferred_element_type=F32)
        up = jnp.dot(rows_ref[...], up_ref[0, :, cols], preferred_element_type=F32)
        act_ref[:, cols] = (gate / (1.0 + jnp.exp(-gate)) * up).astype(BF16)

    for n in range(width // tile):
        made = jnp.dot(
            act_ref[...], down_ref[0, :, n * tile : (n + 1) * tile], preferred_element_type=F32
        ).astype(BF16)
        for jj in range(tile // 128):
            j = n * (tile // 128) + jj
            for g in range(groups):
                for s in range(cap):
                    turned[g, j * 16 : (j + 1) * 16, s * 128 : (s + 1) * 128] = made[
                        s * peers + g * 16 : s * peers + g * 16 + 16, jj * 128 : (jj + 1) * 128
                    ]

    for g in range(groups):
        out_ref[g * 16 : (g + 1) * 16] = (
            jnp.dot(swap, turned[g], preferred_element_type=F32)
            .astype(BF16)
            .reshape(16, per, cap * 128)
        )


def combine_kernel(routed_ref, slots_ref, weights_ref, back_ref, out_ref, wide_ref):
    top, rows = routed_ref.shape
    per = back_ref.shape[1]
    for t in range(rows):
        total = jnp.zeros((per, 128), F32)
        for k in range(top):
            slot = pl.multiple_of(slots_ref[k, t] * 128, 128)
            tile = back_ref[routed_ref[k, t], :, pl.ds(slot, 128)]
            total = total + weights_ref[k, t] * tile.astype(F32)
        wide_ref[t * per : (t + 1) * per, :] = total
    for j in range(per):
        out_ref[:, j * 128 : (j + 1) * 128] = wide_ref[pl.ds(j, rows, stride=per), :].astype(
            out_ref.dtype
        )


def shards(
    ys,
    attn_queries,
    attn_keys,
    attn_values,
    head_gain,
    out_weight,
    residual_in,
    norm_gain,
    routed_experts,
    gate_weights,
    expert_gate,
    expert_up,
    expert_down,
):
    rows, local = attn_queries.shape
    hd = head_gain.shape[0]
    heads = local // hd
    width = out_weight.shape[1]
    seqs = lax.axis_size("seq")
    parts = lax.axis_size("head")
    xs, zs = seqs // ys, parts // 2
    peers = seqs * parts
    hidden = expert_gate.shape[2]
    own_rows, top = routed_experts.shape
    per = width // 128
    cap = CAP

    state_shape = (heads, hd, hd)
    totals, queries, keys, values = pl.pallas_call(
        functools.partial(totals_kernel, heads, hd),
        out_shape=(jax.ShapeDtypeStruct(state_shape, BF16),)
        + (jax.ShapeDtypeStruct((rows, local), F32),) * 3,
        in_specs=[HB] * 3,
        out_specs=(VM,) * 4,
        scratch_shapes=[pltpu.SemaphoreType.DMA((3,))],
        compiler_params=params(2),
        name="totals",
    )(*(in_hbm(part) for part in (attn_queries, attn_keys, attn_values)))

    from_y = [
        lax.ppermute(
            totals, "seq", [(i, i ^ k) for i in range(seqs)]
        )
        for k in range(1, ys)
    ]
    within = pl.pallas_call(
        functools.partial(within_kernel, heads, hd),
        out_shape=jax.ShapeDtypeStruct((rows, local), F32),
        in_specs=[VM] * 3,
        out_specs=VM,
        compiler_params=params(2),
        cost_estimate=cost(12 * heads * rows * rows * hd * 2, 16 * rows * local),
        name="within",
    )(queries, keys, values)
    routed = routed_experts.T
    slots, tokens = pl.pallas_call(
        functools.partial(routing_kernel, cap),
        out_shape=(
            jax.ShapeDtypeStruct((top, own_rows), jnp.int32),
            jax.ShapeDtypeStruct((8, peers), jnp.int32),
        ),
        in_specs=[VM],
        out_specs=(VM, VM),
        compiler_params=params(2),
        name="routing",
    )(routed)

    plane, base = pl.pallas_call(
        plane_kernel,
        out_shape=(
            jax.ShapeDtypeStruct(state_shape, BF16),
            jax.ShapeDtypeStruct(state_shape, F32),
        ),
        in_specs=[VM] * ys + [pl.BlockSpec(memory_space=pl.ANY)],
        out_specs=(VM, VM),
        compiler_params=params(2),
        name="plane",
    )(totals, *from_y, within)
    from_x = [
        lax.ppermute(plane, "seq", [(i, i ^ (k * ys)) for i in range(seqs)])
        for k in range(1, xs)
    ]

    normed, theirs = pl.pallas_call(
        functools.partial(project_kernel, heads, hd, parts, ys),
        out_shape=(
            jax.ShapeDtypeStruct((parts, own_rows, local), BF16),
            jax.ShapeDtypeStruct((zs, own_rows, width), BF16),
        ),
        in_specs=[VM] * 8,
        out_specs=(VM, VM),
        compiler_params=params(2),
        name="project",
    )(
        queries, within, base, *from_x, head_gain.reshape(1, hd), out_weight
    )
    got = lax.ppermute(theirs, "head", [(i, i ^ 1) for i in range(parts)])
    mine = pl.pallas_call(
        keep_kernel,
        out_shape=jax.ShapeDtypeStruct((zs, own_rows, width), F32),
        in_specs=[VM, VM],
        out_specs=VM,
        compiler_params=params(2),
        name="keep",
    )(normed, out_weight)
    blocks = pl.pallas_call(
        functools.partial(pair_kernel, zs),
        out_shape=tuple(
            jax.ShapeDtypeStruct((own_rows, width), F32 if k == 0 else BF16) for k in range(zs)
        ),
        in_specs=[VM, VM],
        out_specs=(VM,) * zs,
        compiler_params=params(2),
        name="pair",
    )(mine, got)
    from_z = [
        lax.ppermute(blocks[k], "head", [(i, i ^ (2 * k)) for i in range(parts)])
        for k in range(1, zs)
    ]

    attn_out, outgoing = pl.pallas_call(
        functools.partial(dispatch_kernel, cap),
        out_shape=(
            jax.ShapeDtypeStruct((own_rows, width), BF16),
            jax.ShapeDtypeStruct((peers, per, cap * 128), BF16),
        ),
        in_specs=[SM] + [VM] * 6,
        out_specs=(VM, VM),
        scratch_shapes=[
            pltpu.VMEM((own_rows * per, 128), F32),
            pltpu.VMEM((own_rows, per, 128), BF16),
        ],
        compiler_params=params(2),
        name="dispatch",
    )(tokens, blocks[0], *from_z, residual_in, norm_gain.reshape(1, width))

    arrived = lax.all_to_all(outgoing, ("seq", "head"), split_axis=0, concat_axis=0, tiled=True)

    produced = pl.pallas_call(
        functools.partial(expert_kernel, cap),
        out_shape=jax.ShapeDtypeStruct((peers, per, cap * 128), BF16),
        in_specs=[VM] * 4,
        out_specs=VM,
        scratch_shapes=[
            pltpu.VMEM((cap * peers, width), BF16),
            pltpu.VMEM((cap * peers, hidden), BF16),
            pltpu.VMEM((peers // 16, per * 16, cap * 128), BF16),
        ],
        compiler_params=params(8),
        name="expert",
    )(arrived, expert_gate, expert_up, expert_down)

    returned = lax.all_to_all(produced, ("seq", "head"), split_axis=0, concat_axis=0, tiled=True)

    moe_out = pl.pallas_call(
        combine_kernel,
        out_shape=jax.ShapeDtypeStruct((own_rows, width), BF16),
        in_specs=[SM, SM, SM, VM],
        out_specs=VM,
        scratch_shapes=[pltpu.VMEM((own_rows * per, 128), F32)],
        compiler_params=params(2),
        name="combine",
    )(routed, slots, gate_weights.T, returned)
    return (attn_out, moe_out)


def solution(mesh):
    return jax.shard_map(
        functools.partial(shards, 4),
        mesh=mesh,
        in_specs=(
            P("seq", "head"),
            P("seq", "head"),
            P("seq", "head"),
            P(),
            P("head", None),
            P(("seq", "head"), None),
            P(),
            P(("seq", "head"), None),
            P(("seq", "head"), None),
            P(("seq", "head"), None, None),
            P(("seq", "head"), None, None),
            P(("seq", "head"), None, None),
        ),
        out_specs=(P(("seq", "head"), None), P(("seq", "head"), None)),
        check_vma=False,
    )
```

```python
import functools
import jax
import jax.numpy as jnp
from jax import lax
from jax.experimental import pallas as pl
from jax.experimental.pallas import tpu as pltpu
from jax.sharding import PartitionSpec as P

EXACT = lax.Precision.HIGHEST
F32 = jnp.float32
BF16 = jnp.bfloat16
CAP = 5
VM = pl.BlockSpec(memory_space=pltpu.VMEM)
SM = pl.BlockSpec(memory_space=pltpu.SMEM)
HB = pl.BlockSpec(memory_space=pltpu.HBM)
MIB = 1 << 20


def in_hbm(array):
    return pltpu.with_memory_space_constraint(array, pltpu.HBM)


def params(mib):
    return pltpu.CompilerParams(vmem_limit_bytes=mib * MIB)


def cost(flops, moved):
    return pl.CostEstimate(flops=flops, bytes_accessed=moved, transcendentals=0)


def totals_kernel(heads, hd, q_hbm, k_hbm, v_hbm, out_ref, q_ref, k_ref, v_ref, sems):
    copies = [
        pltpu.make_async_copy(src, dst, sems.at[n])
        for n, (src, dst) in enumerate([(k_hbm, k_ref), (v_hbm, v_ref), (q_hbm, q_ref)])
    ]
    for copy in copies:
        copy.start()
    copies[0].wait()
    copies[1].wait()
    for h in range(heads):
        cols = slice(h * hd, (h + 1) * hd)
        out_ref[h] = lax.dot_general(
            k_ref[:, cols], v_ref[:, cols], (((0,), (0,)), ((), ())),
            precision=EXACT, preferred_element_type=F32,
        ).astype(BF16)
    copies[2].wait()


def within_kernel(heads, hd, q_ref, k_ref, v_ref, out_ref):
    rows = q_ref.shape[0]
    keep = lax.broadcasted_iota(jnp.int32, (rows, rows), 0) >= lax.broadcasted_iota(
        jnp.int32, (rows, rows), 1
    )
    for h in range(heads):
        cols = slice(h * hd, (h + 1) * hd)
        scores = lax.dot_general(
            q_ref[:, cols], k_ref[:, cols], (((1,), (1,)), ((), ())),
            precision=EXACT, preferred_element_type=F32,
        )
        scores = jnp.where(keep, scores, 0.0)
        out_ref[:, cols] = jnp.dot(
            scores, v_ref[:, cols], precision=EXACT, preferred_element_type=F32
        )


def plane_kernel(ys, own_ref, *refs):
    others = (len(refs) - 2) // 2
    parts, sent, base_ref = refs[:others], refs[-1 - others : -1], refs[-1]
    seq = lax.axis_index("seq")
    x, y = lax.div(seq, ys), lax.rem(seq, ys)
    y_first = lax.rem(lax.axis_index("head"), 2) == 0
    first = jnp.where(y_first, y, x)
    second = jnp.where(y_first, x, y)
    own = own_ref[...].astype(F32)
    total = own
    before = jnp.zeros(own_ref.shape, F32)
    for k, part in enumerate(parts, 1):
        wide = part[...].astype(F32)
        total = total + wide
        before = before + jnp.where((first ^ k) < first, wide, 0.0)
    base_ref[...] = before
    later = jnp.where(y_first, total, before + own)
    sooner = jnp.where(y_first, jnp.zeros_like(before), before)
    for k, out in enumerate(sent, 1):
        out[...] = jnp.where((second ^ k) > second, later, sooner).astype(BF16)


def project_kernel(
    heads, hd, parts, q_ref, in_ref, base_ref, s1_ref, s2_ref, s3_ref, gain_ref, w_ref,
    normed_ref, theirs_ref,
):
    rows = q_ref.shape[0]
    step = rows // parts
    core = lax.rem(lax.axis_index("head"), 2)
    gain = gain_ref[...]
    for h in range(heads):
        cols = slice(h * hd, (h + 1) * hd)
        state = base_ref[h]
        for part in (s1_ref, s2_ref, s3_ref):
            state = state + part[h].astype(F32)
        att = in_ref[:, cols] + jnp.dot(
            q_ref[:, cols], state, precision=EXACT, preferred_element_type=F32
        )
        mean = jnp.mean(att * att, axis=-1, keepdims=True)
        norm = (att * lax.rsqrt(mean + 1e-06) * gain).astype(BF16)
        normed_ref[:, :, cols] = norm.reshape(parts, step, hd)
    theirs_ref[...] = projected(normed_ref, w_ref, 1 - core).astype(BF16)


def projected(normed_ref, w_ref, which):
    half = normed_ref.shape[0] // 2
    picked = jnp.concatenate([normed_ref[2 * z + which] for z in range(half)], axis=0)
    made = jnp.dot(picked, w_ref[...], preferred_element_type=F32)
    return made.reshape(half, normed_ref.shape[1], w_ref.shape[1])


def keep_kernel(normed_ref, w_ref, mine_ref):
    mine_ref[...] = projected(normed_ref, w_ref, lax.rem(lax.axis_index("head"), 2))


def pair_kernel(zs, mine_ref, got_ref, *outs):
    z = lax.div(lax.axis_index("head"), 2)
    for k in range(zs):
        block = z ^ k
        total = mine_ref[block] + got_ref[block].astype(F32)
        outs[k][...] = total.astype(outs[k].dtype)


def routing_kernel(cap, routed_ref, slots_ref, tokens_ref):
    routed = routed_ref[...]
    top, rows = routed.shape
    experts = tokens_ref.shape[1]
    expert = lax.broadcasted_iota(jnp.int32, (experts, rows), 0)
    named = [expert == routed[k : k + 1, :] for k in range(top)]
    member = jnp.zeros((experts, rows), F32)
    for hit in named:
        member = jnp.where(hit, 1.0, member)
    earlier_token = lax.broadcasted_iota(jnp.int32, (rows, rows), 0) < lax.broadcasted_iota(
        jnp.int32, (rows, rows), 1
    )
    earlier = jnp.dot(
        member, earlier_token.astype(F32), precision=EXACT, preferred_element_type=F32
    )
    for k in range(top):
        place = jnp.sum(jnp.where(named[k], earlier, 0.0), axis=0, keepdims=True)
        slots_ref[k : k + 1, :] = place.astype(jnp.int32)
    token = lax.broadcasted_iota(jnp.int32, (8, rows), 1).astype(F32)
    for s in range(cap):
        here = jnp.where((member > 0.5) & (earlier == float(s)), 1.0, 0.0)
        found = lax.dot_general(
            token, here, (((1,), (1,)), ((), ())), precision=EXACT, preferred_element_type=F32
        )
        tokens_ref[s : s + 1, :] = found[0:1, :].astype(jnp.int32)


def dispatch_kernel(
    cap, tokens_hbm, o0_ref, o1_ref, o2_ref, o3_ref, res_ref, gain_ref, attn_ref, out_ref,
    wide_ref, tile_ref, tokens_ref, sem,
):
    rows, width = res_ref.shape
    per = width // 128
    fetch = pltpu.make_async_copy(tokens_hbm, tokens_ref, sem)
    fetch.start()
    total = (
        o0_ref[...] + o1_ref[...].astype(F32) + o2_ref[...].astype(F32) + o3_ref[...].astype(F32)
    )
    attn = total.astype(BF16)
    attn_ref[...] = attn
    mixed = res_ref[...].astype(F32) + attn.astype(F32)
    mean = jnp.mean(mixed * mixed, axis=-1, keepdims=True)
    normed = mixed * lax.rsqrt(mean + 1e-06) * gain_ref[...]
    for j in range(per):
        wide_ref[pl.ds(j, rows, stride=per), :] = normed[:, j * 128 : (j + 1) * 128]
    tile_ref[...] = wide_ref[...].astype(BF16).reshape(rows, per, 128)

    fetch.wait()
    for d in range(out_ref.shape[0]):
        for s in range(cap):
            out_ref[d, :, s * 128 : (s + 1) * 128] = tile_ref[tokens_ref[s, d]]


def expert_kernel(
    cap, in_ref, gate_ref, up_ref, down_ref, out_ref, rows_ref, act_ref, turned
):
    peers, per, _ = in_ref.shape
    groups = peers // 16
    span = per * 16
    width = rows_ref.shape[1]
    hidden = act_ref.shape[1]
    tile = 256

    to = lax.broadcasted_iota(jnp.int32, (span, span), 0)
    fro = lax.broadcasted_iota(jnp.int32, (span, span), 1)
    swap = (fro == (to & 15) * 16 + (to >> 4)).astype(BF16)

    for g in range(groups):
        flat = in_ref[g * 16 : (g + 1) * 16].reshape(span, cap * 128)
        moved = jnp.dot(swap, flat, preferred_element_type=F32).astype(BF16)
        for j in range(per):
            for s in range(cap):
                rows_ref[s * peers + g * 16 : s * peers + g * 16 + 16, j * 128 : (j + 1) * 128] = (
                    moved[j * 16 : (j + 1) * 16, s * 128 : (s + 1) * 128]
                )

    for n in range(hidden // tile):
        cols = slice(n * tile, (n + 1) * tile)
        gate = jnp.dot(rows_ref[...], gate_ref[0, :, cols], preferred_element_type=F32)
        up = jnp.dot(rows_ref[...], up_ref[0, :, cols], preferred_element_type=F32)
        act_ref[:, cols] = (gate / (1.0 + jnp.exp(-gate)) * up).astype(BF16)

    for n in range(width // tile):
        made = jnp.dot(
            act_ref[...], down_ref[0, :, n * tile : (n + 1) * tile], preferred_element_type=F32
        ).astype(BF16)
        for jj in range(tile // 128):
            j = n * (tile // 128) + jj
            for g in range(groups):
                for s in range(cap):
                    turned[g, j * 16 : (j + 1) * 16, s * 128 : (s + 1) * 128] = made[
                        s * peers + g * 16 : s * peers + g * 16 + 16, jj * 128 : (jj + 1) * 128
                    ]

    for g in range(groups):
        out_ref[g * 16 : (g + 1) * 16] = (
            jnp.dot(swap, turned[g], preferred_element_type=F32)
            .astype(BF16)
            .reshape(16, per, cap * 128)
        )


def combine_kernel(routed_ref, slots_ref, weights_ref, back_ref, out_ref, wide_ref):
    top, rows = routed_ref.shape
    per = back_ref.shape[1]
    for t in range(rows):
        total = jnp.zeros((per, 128), F32)
        for k in range(top):
            slot = pl.multiple_of(slots_ref[k, t] * 128, 128)
            tile = back_ref[routed_ref[k, t], :, pl.ds(slot, 128)]
            total = total + weights_ref[k, t] * tile.astype(F32)
        wide_ref[t * per : (t + 1) * per, :] = total
    for j in range(per):
        out_ref[:, j * 128 : (j + 1) * 128] = wide_ref[pl.ds(j, rows, stride=per), :].astype(
            out_ref.dtype
        )


def shards(
    ys,
    attn_queries,
    attn_keys,
    attn_values,
    head_gain,
    out_weight,
    residual_in,
    norm_gain,
    routed_experts,
    gate_weights,
    expert_gate,
    expert_up,
    expert_down,
):
    rows, local = attn_queries.shape
    hd = head_gain.shape[0]
    heads = local // hd
    width = out_weight.shape[1]
    seqs = lax.axis_size("seq")
    parts = lax.axis_size("head")
    zs = parts // 2
    peers = seqs * parts
    hidden = expert_gate.shape[2]
    own_rows, top = routed_experts.shape
    per = width // 128
    cap = CAP

    state_shape = (heads, hd, hd)
    totals, queries, keys, values = pl.pallas_call(
        functools.partial(totals_kernel, heads, hd),
        out_shape=(jax.ShapeDtypeStruct(state_shape, BF16),)
        + (jax.ShapeDtypeStruct((rows, local), F32),) * 3,
        in_specs=[HB] * 3,
        out_specs=(VM,) * 4,
        scratch_shapes=[pltpu.SemaphoreType.DMA((3,))],
        compiler_params=params(2),
        name="totals",
    )(*(in_hbm(part) for part in (attn_queries, attn_keys, attn_values)))

    def exchange(value, k, turn):
        pairs = []
        for device in range(peers):
            along_y = (device % 2 == 0) == (turn == 0)
            pairs.append((device, device ^ (k * parts * (1 if along_y else ys))))
        return lax.ppermute(value, ("seq", "head"), pairs)

    first = [exchange(totals, k, 0) for k in range(1, ys)]
    within = pl.pallas_call(
        functools.partial(within_kernel, heads, hd),
        out_shape=jax.ShapeDtypeStruct((rows, local), F32),
        in_specs=[VM] * 3,
        out_specs=VM,
        compiler_params=params(2),
        cost_estimate=cost(12 * heads * rows * rows * hd * 2, 16 * rows * local),
        name="within",
    )(queries, keys, values)
    routed = routed_experts.T
    slots, tokens = pl.pallas_call(
        functools.partial(routing_kernel, cap),
        out_shape=(
            jax.ShapeDtypeStruct((top, own_rows), jnp.int32),
            jax.ShapeDtypeStruct((8, peers), jnp.int32),
        ),
        in_specs=[VM],
        out_specs=(VM, VM),
        compiler_params=params(2),
        name="routing",
    )(routed)

    *sent, base = pl.pallas_call(
        functools.partial(plane_kernel, ys),
        out_shape=(jax.ShapeDtypeStruct(state_shape, BF16),) * (ys - 1)
        + (jax.ShapeDtypeStruct(state_shape, F32),),
        in_specs=[VM] * ys + [pl.BlockSpec(memory_space=pl.ANY)],
        out_specs=(VM,) * ys,
        compiler_params=params(4),
        name="plane",
    )(totals, *first, within)
    second = [exchange(value, k, 1) for k, value in enumerate(sent, 1)]

    normed, theirs = pl.pallas_call(
        functools.partial(project_kernel, heads, hd, parts),
        out_shape=(
            jax.ShapeDtypeStruct((parts, own_rows, local), BF16),
            jax.ShapeDtypeStruct((zs, own_rows, width), BF16),
        ),
        in_specs=[VM] * 8,
        out_specs=(VM, VM),
        compiler_params=params(2),
        name="project",
    )(
        queries, within, base, *second, head_gain.reshape(1, hd), out_weight
    )
    got = lax.ppermute(theirs, "head", [(i, i ^ 1) for i in range(parts)])
    mine = pl.pallas_call(
        keep_kernel,
        out_shape=jax.ShapeDtypeStruct((zs, own_rows, width), F32),
        in_specs=[VM, VM],
        out_specs=VM,
        compiler_params=params(2),
        name="keep",
    )(normed, out_weight)
    blocks = pl.pallas_call(
        functools.partial(pair_kernel, zs),
        out_shape=tuple(
            jax.ShapeDtypeStruct((own_rows, width), F32 if k == 0 else BF16) for k in range(zs)
        ),
        in_specs=[VM, VM],
        out_specs=(VM,) * zs,
        compiler_params=params(2),
        name="pair",
    )(mine, got)
    from_z = [
        lax.ppermute(blocks[k], "head", [(i, i ^ (2 * k)) for i in range(parts)])
        for k in range(1, zs)
    ]

    attn_out, outgoing = pl.pallas_call(
        functools.partial(dispatch_kernel, cap),
        out_shape=(
            jax.ShapeDtypeStruct((own_rows, width), BF16),
            jax.ShapeDtypeStruct((peers, per, cap * 128), BF16),
        ),
        in_specs=[pl.BlockSpec(memory_space=pl.ANY)] + [VM] * 6,
        out_specs=(VM, VM),
        scratch_shapes=[
            pltpu.VMEM((own_rows * per, 128), F32),
            pltpu.VMEM((own_rows, per, 128), BF16),
            pltpu.SMEM((8, peers), jnp.int32),
            pltpu.SemaphoreType.DMA,
        ],
        compiler_params=params(2),
        name="dispatch",
    )(tokens, blocks[0], *from_z, residual_in, norm_gain.reshape(1, width))

    arrived = lax.all_to_all(outgoing, ("seq", "head"), split_axis=0, concat_axis=0, tiled=True)

    produced = pl.pallas_call(
        functools.partial(expert_kernel, cap),
        out_shape=jax.ShapeDtypeStruct((peers, per, cap * 128), BF16),
        in_specs=[VM] * 4,
        out_specs=VM,
        scratch_shapes=[
            pltpu.VMEM((cap * peers, width), BF16),
            pltpu.VMEM((cap * peers, hidden), BF16),
            pltpu.VMEM((peers // 16, per * 16, cap * 128), BF16),
        ],
        compiler_params=params(8),
        name="expert",
    )(arrived, expert_gate, expert_up, expert_down)

    returned = lax.all_to_all(produced, ("seq", "head"), split_axis=0, concat_axis=0, tiled=True)

    moe_out = pl.pallas_call(
        combine_kernel,
        out_shape=jax.ShapeDtypeStruct((own_rows, width), BF16),
        in_specs=[SM, SM, SM, VM],
        out_specs=VM,
        scratch_shapes=[pltpu.VMEM((own_rows * per, 128), F32)],
        compiler_params=params(2),
        name="combine",
    )(routed, slots, gate_weights.T, returned)
    return (attn_out, moe_out)


def solution(mesh):
    return jax.shard_map(
        functools.partial(shards, 4),
        mesh=mesh,
        in_specs=(
            P("seq", "head"),
            P("seq", "head"),
            P("seq", "head"),
            P(),
            P("head", None),
            P(("seq", "head"), None),
            P(),
            P(("seq", "head"), None),
            P(("seq", "head"), None),
            P(("seq", "head"), None, None),
            P(("seq", "head"), None, None),
            P(("seq", "head"), None, None),
        ),
        out_specs=(P(("seq", "head"), None), P(("seq", "head"), None)),
        check_vma=False,
    )
```

```python
import functools
import jax
import jax.numpy as jnp
from jax import lax
from jax.experimental import pallas as pl
from jax.experimental.pallas import tpu as pltpu
from jax.sharding import PartitionSpec as P

EXACT = lax.Precision.HIGHEST
F32 = jnp.float32
BF16 = jnp.bfloat16
CAP = 5
VM = pl.BlockSpec(memory_space=pltpu.VMEM)
SM = pl.BlockSpec(memory_space=pltpu.SMEM)
HB = pl.BlockSpec(memory_space=pltpu.HBM)
MIB = 1 << 20


def in_hbm(array):
    return pltpu.with_memory_space_constraint(array, pltpu.HBM)


def params(mib):
    return pltpu.CompilerParams(vmem_limit_bytes=mib * MIB)


def cost(flops, moved):
    return pl.CostEstimate(flops=flops, bytes_accessed=moved, transcendentals=0)


def totals_kernel(heads, hd, q_hbm, k_hbm, v_hbm, out_ref, q_ref, k_ref, v_ref, sems):
    copies = [
        pltpu.make_async_copy(src, dst, sems.at[n])
        for n, (src, dst) in enumerate([(k_hbm, k_ref), (v_hbm, v_ref), (q_hbm, q_ref)])
    ]
    for copy in copies:
        copy.start()
    copies[0].wait()
    copies[1].wait()
    for h in range(heads):
        cols = slice(h * hd, (h + 1) * hd)
        out_ref[h] = lax.dot_general(
            k_ref[:, cols], v_ref[:, cols], (((0,), (0,)), ((), ())),
            precision=EXACT, preferred_element_type=F32,
        ).astype(BF16)
    copies[2].wait()


def within_kernel(heads, hd, q_ref, k_ref, v_ref, out_ref):
    rows = q_ref.shape[0]
    keep = lax.broadcasted_iota(jnp.int32, (rows, rows), 0) >= lax.broadcasted_iota(
        jnp.int32, (rows, rows), 1
    )
    for h in range(heads):
        cols = slice(h * hd, (h + 1) * hd)
        scores = lax.dot_general(
            q_ref[:, cols], k_ref[:, cols], (((1,), (1,)), ((), ())),
            precision=EXACT, preferred_element_type=F32,
        )
        scores = jnp.where(keep, scores, 0.0)
        out_ref[:, cols] = jnp.dot(
            scores, v_ref[:, cols], precision=EXACT, preferred_element_type=F32
        )


def plane_kernel(ys, own_ref, *refs):
    others = (len(refs) - 2) // 2
    parts, sent, base_ref = refs[:others], refs[-1 - others : -1], refs[-1]
    seq = lax.axis_index("seq")
    x, y = lax.div(seq, ys), lax.rem(seq, ys)
    y_first = lax.rem(lax.axis_index("head"), 2) == 0
    first = jnp.where(y_first, y, x)
    second = jnp.where(y_first, x, y)
    own = own_ref[...].astype(F32)
    total = own
    before = jnp.zeros(own_ref.shape, F32)
    for k, part in enumerate(parts, 1):
        wide = part[...].astype(F32)
        total = total + wide
        before = before + jnp.where((first ^ k) < first, wide, 0.0)
    base_ref[...] = before
    later = jnp.where(y_first, total, before + own)
    sooner = jnp.where(y_first, jnp.zeros_like(before), before)
    for k, out in enumerate(sent, 1):
        out[...] = jnp.where((second ^ k) > second, later, sooner).astype(BF16)


def normed_kernel(
    heads, hd, parts, q_ref, in_ref, base_ref, s1_ref, s2_ref, s3_ref, gain_ref, mine_ref, theirs_ref,
):
    rows = q_ref.shape[0]
    step = rows // parts
    core = lax.rem(lax.axis_index("head"), 2)
    gain = gain_ref[...]
    for h in range(heads):
        cols = slice(h * hd, (h + 1) * hd)
        state = base_ref[h]
        for part in (s1_ref, s2_ref, s3_ref):
            state = state + part[h].astype(F32)
        att = in_ref[:, cols] + jnp.dot(
            q_ref[:, cols], state, precision=EXACT, preferred_element_type=F32
        )
        mean = jnp.mean(att * att, axis=-1, keepdims=True)
        norm = (att * lax.rsqrt(mean + 1e-06) * gain).astype(BF16)
        blocks = norm.reshape(parts // 2, 2, step, hd)
        even, odd = blocks[:, 0], blocks[:, 1]
        mine_ref[:, :, cols] = jnp.where(core == 0, even, odd)
        theirs_ref[:, :, cols] = jnp.where(core == 0, odd, even)


def projected(normed_ref, w_ref):
    zs, step, depth = normed_ref.shape
    made = jnp.dot(
        normed_ref[...].reshape(zs * step, depth), w_ref[...], preferred_element_type=F32
    )
    return made.reshape(zs, step, w_ref.shape[1])


def keep_kernel(normed_ref, w_ref, mine_ref):
    mine_ref[...] = projected(normed_ref, w_ref)


def pair_kernel(zs, mine_ref, got_ref, w_ref, *refs):
    outs, sum_ref = refs[:-1], refs[-1]
    z = lax.div(lax.axis_index("head"), 2)
    sum_ref[...] = mine_ref[...] + projected(got_ref, w_ref)
    for k in range(zs):
        outs[k][...] = sum_ref[z ^ k].astype(outs[k].dtype)


def routing_kernel(cap, routed_ref, slots_ref, tokens_ref):
    routed = routed_ref[...]
    top, rows = routed.shape
    experts = tokens_ref.shape[1]
    expert = lax.broadcasted_iota(jnp.int32, (experts, rows), 0)
    named = [expert == routed[k : k + 1, :] for k in range(top)]
    member = jnp.zeros((experts, rows), F32)
    for hit in named:
        member = jnp.where(hit, 1.0, member)
    earlier_token = lax.broadcasted_iota(jnp.int32, (rows, rows), 0) < lax.broadcasted_iota(
        jnp.int32, (rows, rows), 1
    )
    earlier = jnp.dot(
        member, earlier_token.astype(F32), precision=EXACT, preferred_element_type=F32
    )
    for k in range(top):
        place = jnp.sum(jnp.where(named[k], earlier, 0.0), axis=0, keepdims=True)
        slots_ref[k : k + 1, :] = place.astype(jnp.int32)
    token = lax.broadcasted_iota(jnp.int32, (8, rows), 1).astype(F32)
    for s in range(cap):
        here = jnp.where((member > 0.5) & (earlier == float(s)), 1.0, 0.0)
        found = lax.dot_general(
            token, here, (((1,), (1,)), ((), ())), precision=EXACT, preferred_element_type=F32
        )
        tokens_ref[s : s + 1, :] = found[0:1, :].astype(jnp.int32)


def dispatch_kernel(
    cap, tokens_hbm, o0_ref, o1_ref, o2_ref, o3_ref, res_ref, gain_ref, attn_ref, out_ref,
    wide_ref, tile_ref, tokens_ref, sem,
):
    rows, width = res_ref.shape
    per = width // 128
    fetch = pltpu.make_async_copy(tokens_hbm, tokens_ref, sem)
    fetch.start()
    total = (
        o0_ref[...] + o1_ref[...].astype(F32) + o2_ref[...].astype(F32) + o3_ref[...].astype(F32)
    )
    attn = total.astype(BF16)
    attn_ref[...] = attn
    mixed = res_ref[...].astype(F32) + attn.astype(F32)
    mean = jnp.mean(mixed * mixed, axis=-1, keepdims=True)
    normed = mixed * lax.rsqrt(mean + 1e-06) * gain_ref[...]
    for j in range(per):
        wide_ref[pl.ds(j, rows, stride=per), :] = normed[:, j * 128 : (j + 1) * 128]
    tile_ref[...] = wide_ref[...].astype(BF16).reshape(rows, per, 128)

    fetch.wait()
    for d in range(out_ref.shape[0]):
        for s in range(cap):
            out_ref[d, :, s * 128 : (s + 1) * 128] = tile_ref[tokens_ref[s, d]]


def expert_kernel(
    cap, in_ref, gate_ref, up_ref, down_ref, out_ref, rows_ref, act_ref, turned
):
    peers, per, _ = in_ref.shape
    groups = peers // 16
    span = per * 16
    width = rows_ref.shape[1]
    hidden = act_ref.shape[1]
    tile = 256

    to = lax.broadcasted_iota(jnp.int32, (span, span), 0)
    fro = lax.broadcasted_iota(jnp.int32, (span, span), 1)
    swap = (fro == (to & 15) * 16 + (to >> 4)).astype(BF16)

    for g in range(groups):
        flat = in_ref[g * 16 : (g + 1) * 16].reshape(span, cap * 128)
        moved = jnp.dot(swap, flat, preferred_element_type=F32).astype(BF16)
        for j in range(per):
            for s in range(cap):
                rows_ref[s * peers + g * 16 : s * peers + g * 16 + 16, j * 128 : (j + 1) * 128] = (
                    moved[j * 16 : (j + 1) * 16, s * 128 : (s + 1) * 128]
                )

    for n in range(hidden // tile):
        cols = slice(n * tile, (n + 1) * tile)
        gate = jnp.dot(rows_ref[...], gate_ref[0, :, cols], preferred_element_type=F32)
        up = jnp.dot(rows_ref[...], up_ref[0, :, cols], preferred_element_type=F32)
        act_ref[:, cols] = (gate / (1.0 + jnp.exp(-gate)) * up).astype(BF16)

    for n in range(width // tile):
        made = jnp.dot(
            act_ref[...], down_ref[0, :, n * tile : (n + 1) * tile], preferred_element_type=F32
        ).astype(BF16)
        for jj in range(tile // 128):
            j = n * (tile // 128) + jj
            for g in range(groups):
                for s in range(cap):
                    turned[g, j * 16 : (j + 1) * 16, s * 128 : (s + 1) * 128] = made[
                        s * peers + g * 16 : s * peers + g * 16 + 16, jj * 128 : (jj + 1) * 128
                    ]

    for g in range(groups):
        out_ref[g * 16 : (g + 1) * 16] = (
            jnp.dot(swap, turned[g], preferred_element_type=F32)
            .astype(BF16)
            .reshape(16, per, cap * 128)
        )


def combine_kernel(routed_ref, slots_ref, weights_ref, back_ref, out_ref, wide_ref):
    top, rows = routed_ref.shape
    per = back_ref.shape[1]
    for t in range(rows):
        total = jnp.zeros((per, 128), F32)
        for k in range(top):
            slot = pl.multiple_of(slots_ref[k, t] * 128, 128)
            tile = back_ref[routed_ref[k, t], :, pl.ds(slot, 128)]
            total = total + weights_ref[k, t] * tile.astype(F32)
        wide_ref[t * per : (t + 1) * per, :] = total
    for j in range(per):
        out_ref[:, j * 128 : (j + 1) * 128] = wide_ref[pl.ds(j, rows, stride=per), :].astype(
            out_ref.dtype
        )


def shards(
    ys,
    attn_queries,
    attn_keys,
    attn_values,
    head_gain,
    out_weight,
    residual_in,
    norm_gain,
    routed_experts,
    gate_weights,
    expert_gate,
    expert_up,
    expert_down,
):
    rows, local = attn_queries.shape
    hd = head_gain.shape[0]
    heads = local // hd
    width = out_weight.shape[1]
    seqs = lax.axis_size("seq")
    parts = lax.axis_size("head")
    zs = parts // 2
    peers = seqs * parts
    hidden = expert_gate.shape[2]
    own_rows, top = routed_experts.shape
    per = width // 128
    cap = CAP

    state_shape = (heads, hd, hd)
    totals, queries, keys, values = pl.pallas_call(
        functools.partial(totals_kernel, heads, hd),
        out_shape=(jax.ShapeDtypeStruct(state_shape, BF16),)
        + (jax.ShapeDtypeStruct((rows, local), F32),) * 3,
        in_specs=[HB] * 3,
        out_specs=(VM,) * 4,
        scratch_shapes=[pltpu.SemaphoreType.DMA((3,))],
        compiler_params=params(2),
        name="totals",
    )(*(in_hbm(part) for part in (attn_queries, attn_keys, attn_values)))

    def exchange(value, k, turn):
        pairs = []
        for device in range(peers):
            along_y = (device % 2 == 0) == (turn == 0)
            pairs.append((device, device ^ (k * parts * (1 if along_y else ys))))
        return lax.ppermute(value, ("seq", "head"), pairs)

    other_weight = lax.ppermute(out_weight, "head", [(i, i ^ 1) for i in range(parts)])
    first = [exchange(totals, k, 0) for k in range(1, ys)]
    within = pl.pallas_call(
        functools.partial(within_kernel, heads, hd),
        out_shape=jax.ShapeDtypeStruct((rows, local), F32),
        in_specs=[VM] * 3,
        out_specs=VM,
        compiler_params=params(2),
        cost_estimate=cost(12 * heads * rows * rows * hd * 2, 16 * rows * local),
        name="within",
    )(queries, keys, values)
    routed = routed_experts.T
    slots, tokens = pl.pallas_call(
        functools.partial(routing_kernel, cap),
        out_shape=(
            jax.ShapeDtypeStruct((top, own_rows), jnp.int32),
            jax.ShapeDtypeStruct((8, peers), jnp.int32),
        ),
        in_specs=[VM],
        out_specs=(VM, VM),
        compiler_params=params(2),
        name="routing",
    )(routed)

    *sent, base = pl.pallas_call(
        functools.partial(plane_kernel, ys),
        out_shape=(jax.ShapeDtypeStruct(state_shape, BF16),) * (ys - 1)
        + (jax.ShapeDtypeStruct(state_shape, F32),),
        in_specs=[VM] * ys + [pl.BlockSpec(memory_space=pl.ANY)],
        out_specs=(VM,) * ys,
        compiler_params=params(4),
        name="plane",
    )(totals, *first, within)
    second = [exchange(value, k, 1) for k, value in enumerate(sent, 1)]

    normed, theirs = pl.pallas_call(
        functools.partial(normed_kernel, heads, hd, parts),
        out_shape=(jax.ShapeDtypeStruct((zs, own_rows, local), BF16),) * 2,
        in_specs=[VM] * 7,
        out_specs=(VM, VM),
        compiler_params=params(2),
        name="normed",
    )(queries, within, base, *second, head_gain.reshape(1, hd))
    got = lax.ppermute(theirs, "head", [(i, i ^ 1) for i in range(parts)])
    mine = pl.pallas_call(
        keep_kernel,
        out_shape=jax.ShapeDtypeStruct((zs, own_rows, width), F32),
        in_specs=[VM, VM],
        out_specs=VM,
        compiler_params=params(2),
        name="keep",
    )(normed, out_weight)
    blocks = pl.pallas_call(
        functools.partial(pair_kernel, zs),
        out_shape=tuple(
            jax.ShapeDtypeStruct((own_rows, width), F32 if k == 0 else BF16) for k in range(zs)
        ),
        in_specs=[VM] * 3,
        out_specs=(VM,) * zs,
        scratch_shapes=[pltpu.VMEM((zs, own_rows, width), F32)],
        compiler_params=params(4),
        name="pair",
    )(mine, got, other_weight)
    from_z = [
        lax.ppermute(blocks[k], "head", [(i, i ^ (2 * k)) for i in range(parts)])
        for k in range(1, zs)
    ]

    attn_out, outgoing = pl.pallas_call(
        functools.partial(dispatch_kernel, cap),
        out_shape=(
            jax.ShapeDtypeStruct((own_rows, width), BF16),
            jax.ShapeDtypeStruct((peers, per, cap * 128), BF16),
        ),
        in_specs=[pl.BlockSpec(memory_space=pl.ANY)] + [VM] * 6,
        out_specs=(VM, VM),
        scratch_shapes=[
            pltpu.VMEM((own_rows * per, 128), F32),
            pltpu.VMEM((own_rows, per, 128), BF16),
            pltpu.SMEM((8, peers), jnp.int32),
            pltpu.SemaphoreType.DMA,
        ],
        compiler_params=params(2),
        name="dispatch",
    )(tokens, blocks[0], *from_z, residual_in, norm_gain.reshape(1, width))

    arrived = lax.all_to_all(outgoing, ("seq", "head"), split_axis=0, concat_axis=0, tiled=True)

    produced = pl.pallas_call(
        functools.partial(expert_kernel, cap),
        out_shape=jax.ShapeDtypeStruct((peers, per, cap * 128), BF16),
        in_specs=[VM] * 4,
        out_specs=VM,
        scratch_shapes=[
            pltpu.VMEM((cap * peers, width), BF16),
            pltpu.VMEM((cap * peers, hidden), BF16),
            pltpu.VMEM((peers // 16, per * 16, cap * 128), BF16),
        ],
        compiler_params=params(8),
        name="expert",
    )(arrived, expert_gate, expert_up, expert_down)

    returned = lax.all_to_all(produced, ("seq", "head"), split_axis=0, concat_axis=0, tiled=True)

    moe_out = pl.pallas_call(
        combine_kernel,
        out_shape=jax.ShapeDtypeStruct((own_rows, width), BF16),
        in_specs=[SM, SM, SM, VM],
        out_specs=VM,
        scratch_shapes=[pltpu.VMEM((own_rows * per, 128), F32)],
        compiler_params=params(2),
        name="combine",
    )(routed, slots, gate_weights.T, returned)
    return (attn_out, moe_out)


def solution(mesh):
    return jax.shard_map(
        functools.partial(shards, 4),
        mesh=mesh,
        in_specs=(
            P("seq", "head"),
            P("seq", "head"),
            P("seq", "head"),
            P(),
            P("head", None),
            P(("seq", "head"), None),
            P(),
            P(("seq", "head"), None),
            P(("seq", "head"), None),
            P(("seq", "head"), None, None),
            P(("seq", "head"), None, None),
            P(("seq", "head"), None, None),
        ),
        out_specs=(P(("seq", "head"), None), P(("seq", "head"), None)),
        check_vma=False,
    )
```

```python
import functools
import jax
import jax.numpy as jnp
from jax import lax
from jax.experimental import pallas as pl
from jax.experimental.pallas import tpu as pltpu
from jax.sharding import PartitionSpec as P

EXACT = lax.Precision.HIGHEST
F32 = jnp.float32
BF16 = jnp.bfloat16
CAP = 5
VM = pl.BlockSpec(memory_space=pltpu.VMEM)
SM = pl.BlockSpec(memory_space=pltpu.SMEM)
HB = pl.BlockSpec(memory_space=pltpu.HBM)
MIB = 1 << 20


def in_hbm(array):
    return pltpu.with_memory_space_constraint(array, pltpu.HBM)


def params(mib):
    return pltpu.CompilerParams(vmem_limit_bytes=mib * MIB)


def cost(flops, moved):
    return pl.CostEstimate(flops=flops, bytes_accessed=moved, transcendentals=0)


def totals_kernel(heads, hd, q_hbm, k_hbm, v_hbm, out_ref, q_ref, k_ref, v_ref, sems):
    copies = [
        pltpu.make_async_copy(src, dst, sems.at[n])
        for n, (src, dst) in enumerate([(k_hbm, k_ref), (v_hbm, v_ref), (q_hbm, q_ref)])
    ]
    for copy in copies:
        copy.start()
    copies[0].wait()
    copies[1].wait()
    for h in range(heads):
        cols = slice(h * hd, (h + 1) * hd)
        out_ref[h] = lax.dot_general(
            k_ref[:, cols], v_ref[:, cols], (((0,), (0,)), ((), ())),
            precision=EXACT, preferred_element_type=F32,
        ).astype(BF16)
    copies[2].wait()


def within_kernel(heads, hd, q_ref, k_ref, v_ref, out_ref):
    rows = q_ref.shape[0]
    keep = lax.broadcasted_iota(jnp.int32, (rows, rows), 0) >= lax.broadcasted_iota(
        jnp.int32, (rows, rows), 1
    )
    for h in range(heads):
        cols = slice(h * hd, (h + 1) * hd)
        scores = lax.dot_general(
            q_ref[:, cols], k_ref[:, cols], (((1,), (1,)), ((), ())),
            precision=EXACT, preferred_element_type=F32,
        )
        scores = jnp.where(keep, scores, 0.0)
        out_ref[:, cols] = jnp.dot(
            scores, v_ref[:, cols], precision=EXACT, preferred_element_type=F32
        )


def plane_kernel(ys, own_ref, *refs):
    others = (len(refs) - 2) // 2
    parts, sent, base_ref = refs[:others], refs[-1 - others : -1], refs[-1]
    seq = lax.axis_index("seq")
    x, y = lax.div(seq, ys), lax.rem(seq, ys)
    y_first = lax.rem(lax.axis_index("head"), 2) == 0
    first = jnp.where(y_first, y, x)
    second = jnp.where(y_first, x, y)
    own = own_ref[...].astype(F32)
    total = own
    before = jnp.zeros(own_ref.shape, F32)
    for k, part in enumerate(parts, 1):
        wide = part[...].astype(F32)
        total = total + wide
        before = before + jnp.where((first ^ k) < first, wide, 0.0)
    base_ref[...] = before
    later = jnp.where(y_first, total, before + own)
    sooner = jnp.where(y_first, jnp.zeros_like(before), before)
    for k, out in enumerate(sent, 1):
        out[...] = jnp.where((second ^ k) > second, later, sooner).astype(BF16)


def normed_kernel(
    heads, hd, parts, q_ref, in_ref, base_ref, s1_ref, s2_ref, s3_ref, gain_ref, mine_ref, theirs_ref,
):
    rows = q_ref.shape[0]
    step = rows // parts
    core = lax.rem(lax.axis_index("head"), 2)
    gain = gain_ref[...]
    for h in range(heads):
        cols = slice(h * hd, (h + 1) * hd)
        state = base_ref[h]
        for part in (s1_ref, s2_ref, s3_ref):
            state = state + part[h].astype(F32)
        att = in_ref[:, cols] + jnp.dot(
            q_ref[:, cols], state, precision=EXACT, preferred_element_type=F32
        )
        mean = jnp.mean(att * att, axis=-1, keepdims=True)
        norm = (att * lax.rsqrt(mean + 1e-06) * gain).astype(BF16)
        blocks = norm.reshape(parts // 2, 2, step, hd)
        even, odd = blocks[:, 0], blocks[:, 1]
        mine_ref[:, :, cols] = jnp.where(core == 0, even, odd)
        theirs_ref[:, :, cols] = jnp.where(core == 0, odd, even)


def projected(normed_ref, w_ref):
    zs, step, depth = normed_ref.shape
    made = jnp.dot(
        normed_ref[...].reshape(zs * step, depth), w_ref[...], preferred_element_type=F32
    )
    return made.reshape(zs, step, w_ref.shape[1])


def keep_kernel(normed_ref, w_ref, mine_ref):
    mine_ref[...] = projected(normed_ref, w_ref)


def pair_kernel(zs, mine_ref, got_ref, w_ref, *refs):
    outs, sum_ref = refs[:-1], refs[-1]
    z = lax.div(lax.axis_index("head"), 2)
    sum_ref[...] = mine_ref[...] + projected(got_ref, w_ref)
    core = lax.rem(lax.axis_index("head"), 2)
    for k in range(zs):
        along = jnp.where(core == 0, k, (zs - k) % zs)
        outs[k][...] = sum_ref[z ^ along].astype(outs[k].dtype)


def routing_kernel(cap, routed_ref, slots_ref, tokens_ref):
    routed = routed_ref[...]
    top, rows = routed.shape
    experts = tokens_ref.shape[1]
    expert = lax.broadcasted_iota(jnp.int32, (experts, rows), 0)
    named = [expert == routed[k : k + 1, :] for k in range(top)]
    member = jnp.zeros((experts, rows), F32)
    for hit in named:
        member = jnp.where(hit, 1.0, member)
    earlier_token = lax.broadcasted_iota(jnp.int32, (rows, rows), 0) < lax.broadcasted_iota(
        jnp.int32, (rows, rows), 1
    )
    earlier = jnp.dot(
        member, earlier_token.astype(F32), precision=EXACT, preferred_element_type=F32
    )
    for k in range(top):
        place = jnp.sum(jnp.where(named[k], earlier, 0.0), axis=0, keepdims=True)
        slots_ref[k : k + 1, :] = place.astype(jnp.int32)
    token = lax.broadcasted_iota(jnp.int32, (8, rows), 1).astype(F32)
    for s in range(cap):
        here = jnp.where((member > 0.5) & (earlier == float(s)), 1.0, 0.0)
        found = lax.dot_general(
            token, here, (((1,), (1,)), ((), ())), precision=EXACT, preferred_element_type=F32
        )
        tokens_ref[s : s + 1, :] = found[0:1, :].astype(jnp.int32)


def dispatch_kernel(
    cap, tokens_hbm, o0_ref, o1_ref, o2_ref, o3_ref, res_ref, gain_ref, attn_ref, out_ref,
    wide_ref, tile_ref, tokens_ref, sem,
):
    rows, width = res_ref.shape
    per = width // 128
    fetch = pltpu.make_async_copy(tokens_hbm, tokens_ref, sem)
    fetch.start()
    total = (
        o0_ref[...] + o1_ref[...].astype(F32) + o2_ref[...].astype(F32) + o3_ref[...].astype(F32)
    )
    attn = total.astype(BF16)
    attn_ref[...] = attn
    mixed = res_ref[...].astype(F32) + attn.astype(F32)
    mean = jnp.mean(mixed * mixed, axis=-1, keepdims=True)
    normed = mixed * lax.rsqrt(mean + 1e-06) * gain_ref[...]
    for j in range(per):
        wide_ref[pl.ds(j, rows, stride=per), :] = normed[:, j * 128 : (j + 1) * 128]
    tile_ref[...] = wide_ref[...].astype(BF16).reshape(rows, per, 128)

    fetch.wait()
    for d in range(out_ref.shape[0]):
        for s in range(cap):
            out_ref[d, :, s * 128 : (s + 1) * 128] = tile_ref[tokens_ref[s, d]]


def expert_kernel(
    cap, in_ref, gate_ref, up_ref, down_ref, out_ref, rows_ref, act_ref, turned
):
    peers, per, _ = in_ref.shape
    groups = peers // 16
    span = per * 16
    width = rows_ref.shape[1]
    hidden = act_ref.shape[1]
    tile = 256

    to = lax.broadcasted_iota(jnp.int32, (span, span), 0)
    fro = lax.broadcasted_iota(jnp.int32, (span, span), 1)
    swap = (fro == (to & 15) * 16 + (to >> 4)).astype(BF16)

    for g in range(groups):
        flat = in_ref[g * 16 : (g + 1) * 16].reshape(span, cap * 128)
        moved = jnp.dot(swap, flat, preferred_element_type=F32).astype(BF16)
        for j in range(per):
            for s in range(cap):
                rows_ref[s * peers + g * 16 : s * peers + g * 16 + 16, j * 128 : (j + 1) * 128] = (
                    moved[j * 16 : (j + 1) * 16, s * 128 : (s + 1) * 128]
                )

    for n in range(hidden // tile):
        cols = slice(n * tile, (n + 1) * tile)
        gate = jnp.dot(rows_ref[...], gate_ref[0, :, cols], preferred_element_type=F32)
        up = jnp.dot(rows_ref[...], up_ref[0, :, cols], preferred_element_type=F32)
        act_ref[:, cols] = (gate / (1.0 + jnp.exp(-gate)) * up).astype(BF16)

    for n in range(width // tile):
        made = jnp.dot(
            act_ref[...], down_ref[0, :, n * tile : (n + 1) * tile], preferred_element_type=F32
        ).astype(BF16)
        for jj in range(tile // 128):
            j = n * (tile // 128) + jj
            for g in range(groups):
                for s in range(cap):
                    turned[g, j * 16 : (j + 1) * 16, s * 128 : (s + 1) * 128] = made[
                        s * peers + g * 16 : s * peers + g * 16 + 16, jj * 128 : (jj + 1) * 128
                    ]

    for g in range(groups):
        out_ref[g * 16 : (g + 1) * 16] = (
            jnp.dot(swap, turned[g], preferred_element_type=F32)
            .astype(BF16)
            .reshape(16, per, cap * 128)
        )


def combine_kernel(routed_ref, slots_ref, weights_ref, back_ref, out_ref, wide_ref):
    top, rows = routed_ref.shape
    per = back_ref.shape[1]
    for t in range(rows):
        total = jnp.zeros((per, 128), F32)
        for k in range(top):
            slot = pl.multiple_of(slots_ref[k, t] * 128, 128)
            tile = back_ref[routed_ref[k, t], :, pl.ds(slot, 128)]
            total = total + weights_ref[k, t] * tile.astype(F32)
        wide_ref[t * per : (t + 1) * per, :] = total
    for j in range(per):
        out_ref[:, j * 128 : (j + 1) * 128] = wide_ref[pl.ds(j, rows, stride=per), :].astype(
            out_ref.dtype
        )


def shards(
    ys,
    attn_queries,
    attn_keys,
    attn_values,
    head_gain,
    out_weight,
    residual_in,
    norm_gain,
    routed_experts,
    gate_weights,
    expert_gate,
    expert_up,
    expert_down,
):
    rows, local = attn_queries.shape
    hd = head_gain.shape[0]
    heads = local // hd
    width = out_weight.shape[1]
    seqs = lax.axis_size("seq")
    parts = lax.axis_size("head")
    zs = parts // 2
    peers = seqs * parts
    hidden = expert_gate.shape[2]
    own_rows, top = routed_experts.shape
    per = width // 128
    cap = CAP

    state_shape = (heads, hd, hd)
    totals, queries, keys, values = pl.pallas_call(
        functools.partial(totals_kernel, heads, hd),
        out_shape=(jax.ShapeDtypeStruct(state_shape, BF16),)
        + (jax.ShapeDtypeStruct((rows, local), F32),) * 3,
        in_specs=[HB] * 3,
        out_specs=(VM,) * 4,
        scratch_shapes=[pltpu.SemaphoreType.DMA((3,))],
        compiler_params=params(2),
        name="totals",
    )(*(in_hbm(part) for part in (attn_queries, attn_keys, attn_values)))

    def exchange(value, k, turn):
        pairs = []
        for device in range(peers):
            along_y = (device % 2 == 0) == (turn == 0)
            pairs.append((device, device ^ (k * parts * (1 if along_y else ys))))
        return lax.ppermute(value, ("seq", "head"), pairs)

    other_weight = lax.ppermute(out_weight, "head", [(i, i ^ 1) for i in range(parts)])
    first = [exchange(totals, k, 0) for k in range(1, ys)]
    within = pl.pallas_call(
        functools.partial(within_kernel, heads, hd),
        out_shape=jax.ShapeDtypeStruct((rows, local), F32),
        in_specs=[VM] * 3,
        out_specs=VM,
        compiler_params=params(2),
        cost_estimate=cost(12 * heads * rows * rows * hd * 2, 16 * rows * local),
        name="within",
    )(queries, keys, values)
    routed = routed_experts.T
    slots, tokens = pl.pallas_call(
        functools.partial(routing_kernel, cap),
        out_shape=(
            jax.ShapeDtypeStruct((top, own_rows), jnp.int32),
            jax.ShapeDtypeStruct((8, peers), jnp.int32),
        ),
        in_specs=[VM],
        out_specs=(VM, VM),
        compiler_params=params(2),
        name="routing",
    )(routed)

    *sent, base = pl.pallas_call(
        functools.partial(plane_kernel, ys),
        out_shape=(jax.ShapeDtypeStruct(state_shape, BF16),) * (ys - 1)
        + (jax.ShapeDtypeStruct(state_shape, F32),),
        in_specs=[VM] * ys + [pl.BlockSpec(memory_space=pl.ANY)],
        out_specs=(VM,) * ys,
        compiler_params=params(4),
        name="plane",
    )(totals, *first, within)
    second = [exchange(value, k, 1) for k, value in enumerate(sent, 1)]

    normed, theirs = pl.pallas_call(
        functools.partial(normed_kernel, heads, hd, parts),
        out_shape=(jax.ShapeDtypeStruct((zs, own_rows, local), BF16),) * 2,
        in_specs=[VM] * 7,
        out_specs=(VM, VM),
        compiler_params=params(2),
        name="normed",
    )(queries, within, base, *second, head_gain.reshape(1, hd))
    got = lax.ppermute(theirs, "head", [(i, i ^ 1) for i in range(parts)])
    mine = pl.pallas_call(
        keep_kernel,
        out_shape=jax.ShapeDtypeStruct((zs, own_rows, width), F32),
        in_specs=[VM, VM],
        out_specs=VM,
        compiler_params=params(2),
        name="keep",
    )(normed, out_weight)
    blocks = pl.pallas_call(
        functools.partial(pair_kernel, zs),
        out_shape=tuple(
            jax.ShapeDtypeStruct((own_rows, width), F32 if k == 0 else BF16) for k in range(zs)
        ),
        in_specs=[VM] * 3,
        out_specs=(VM,) * zs,
        scratch_shapes=[pltpu.VMEM((zs, own_rows, width), F32)],
        compiler_params=params(4),
        name="pair",
    )(mine, got, other_weight)
    from_z = [
        lax.ppermute(
            blocks[k], "head", [(i, i ^ (2 * (k if i % 2 == 0 else zs - k))) for i in range(parts)]
        )
        for k in range(1, zs)
    ]

    attn_out, outgoing = pl.pallas_call(
        functools.partial(dispatch_kernel, cap),
        out_shape=(
            jax.ShapeDtypeStruct((own_rows, width), BF16),
            jax.ShapeDtypeStruct((peers, per, cap * 128), BF16),
        ),
        in_specs=[pl.BlockSpec(memory_space=pl.ANY)] + [VM] * 6,
        out_specs=(VM, VM),
        scratch_shapes=[
            pltpu.VMEM((own_rows * per, 128), F32),
            pltpu.VMEM((own_rows, per, 128), BF16),
            pltpu.SMEM((8, peers), jnp.int32),
            pltpu.SemaphoreType.DMA,
        ],
        compiler_params=params(2),
        name="dispatch",
    )(tokens, blocks[0], *from_z, residual_in, norm_gain.reshape(1, width))

    arrived = lax.all_to_all(outgoing, ("seq", "head"), split_axis=0, concat_axis=0, tiled=True)

    produced = pl.pallas_call(
        functools.partial(expert_kernel, cap),
        out_shape=jax.ShapeDtypeStruct((peers, per, cap * 128), BF16),
        in_specs=[VM] * 4,
        out_specs=VM,
        scratch_shapes=[
            pltpu.VMEM((cap * peers, width), BF16),
            pltpu.VMEM((cap * peers, hidden), BF16),
            pltpu.VMEM((peers // 16, per * 16, cap * 128), BF16),
        ],
        compiler_params=params(8),
        name="expert",
    )(arrived, expert_gate, expert_up, expert_down)

    returned = lax.all_to_all(produced, ("seq", "head"), split_axis=0, concat_axis=0, tiled=True)

    moe_out = pl.pallas_call(
        combine_kernel,
        out_shape=jax.ShapeDtypeStruct((own_rows, width), BF16),
        in_specs=[SM, SM, SM, VM],
        out_specs=VM,
        scratch_shapes=[pltpu.VMEM((own_rows * per, 128), F32)],
        compiler_params=params(2),
        name="combine",
    )(routed, slots, gate_weights.T, returned)
    return (attn_out, moe_out)


def solution(mesh):
    return jax.shard_map(
        functools.partial(shards, 4),
        mesh=mesh,
        in_specs=(
            P("seq", "head"),
            P("seq", "head"),
            P("seq", "head"),
            P(),
            P("head", None),
            P(("seq", "head"), None),
            P(),
            P(("seq", "head"), None),
            P(("seq", "head"), None),
            P(("seq", "head"), None, None),
            P(("seq", "head"), None, None),
            P(("seq", "head"), None, None),
        ),
        out_specs=(P(("seq", "head"), None), P(("seq", "head"), None)),
        check_vma=False,
    )
```
